256 devices in a mesh: view: 8 (over x, z_lo), gz: 32 (over y, z_hi, core).
Axes of the slice: x: 4, y: 4, z: 8 (z_hi: 4, z_lo: 2; z = z_hi * 2 + z_lo), core: 2. Of those that a mesh axis runs over, the one named last changes fastest.
Arguments:
- views_data: bfloat16 [8, 1024, 128, 256], P('view', 'gz'), may hold values from 0.29882812 to 3
- psf: float32 [8, 3, 31], P('view'), may hold values from 0.02 to 1
- start: float32 [1024, 128, 256], P('gz'), may hold values from 0.05 to 12, as said below
Outputs:
- estimate: float32 [1024, 128, 256], P('gz')
The draws below stay inside these ranges and needn't reach their ends.
Inputs may be any that keep to these rules, and one draw needn't show every extreme that they name: `start`: positive.
All inputs are finite; a program needn't handle non-finite values.
Results may differ from the reference program's by a relative error of at most 0.0003.
Values may be sent and summed in bfloat16 or wider, within the bound.
No kernel may reach another device: no remote copies, remote signals or barrier semaphores. Data moves between devices by JAX's collectives and lax.ppermute only.
A program may use at most 128 MiB of HBM per device.

```python
import math
import jax
import jax.numpy as jnp
from jax import lax

NX = 128
NY = 256
RADIUS = 15
TAPS = 31
ITERS = 2
VIEWS = 8
NZ = 1024


def draw_start(key, part):
    key = jax.random.fold_in(key, 7)
    plane_key = jax.random.fold_in(key, 1)
    cell_key = jax.random.fold_in(key, 2)
    plane_log = jax.random.uniform(plane_key, (NZ, 1, 1), jnp.float32, math.log(0.2), math.log(5.0))
    cells = jnp.exp(jax.random.uniform(cell_key, (NZ, NX, NY), jnp.float32, math.log(0.5), math.log(2.0)))
    return (jnp.exp(plane_log) * cells).astype(jnp.float32)


def steps_of(own_key, dims, split, smallest, largest):
    gain, own = 1.0, jax.random.fold_in(own_key, 6)
    for position, shards_of in split:
        draws = jnp.exp(jax.random.uniform(jax.random.fold_in(own, position), (shards_of,), jnp.float32, smallest / len(split), largest / len(split)))
        gain = gain * jnp.repeat(draws, dims[position] // shards_of).reshape([-1 if axis == position else 1 for axis in range(len(dims))])
    return gain


def setup_inputs(seed: int = 0) -> dict:
    key_of = jax.random.split(jax.random.key(seed), 4)
    return {
        "views_data": jnp.clip(jnp.exp(math.log(3.0) - 2.306499 * jax.random.uniform(key_of[0], (VIEWS, NZ, NX, NY), jnp.float32) ** steps_of(key_of[0], (VIEWS, NZ, NX, NY), ((0, 8), (1, 32)), -0.2, 0.2)), 0.29882812, 3.0).astype(jnp.bfloat16),
        "psf": jnp.clip(jnp.exp(math.log(1.0) - 3.912023 * jax.random.uniform(key_of[1], (VIEWS, 3, TAPS), jnp.float32) ** steps_of(key_of[1], (VIEWS, 3, TAPS), ((0, 8),), -0.2, 0.2)), 0.02, 1.0),
        "start": draw_start(jax.random.fold_in(key_of[3], 71), 0),
    }


def band_matrix(kernel_row, n_out, n_in, offset, direction):
    out_index = jnp.arange(n_out, dtype=jnp.int32)[:, None]
    in_index = jnp.arange(n_in, dtype=jnp.int32)[None, :]
    tap_index = direction * (in_index - out_index - offset) + RADIUS
    one_hot = (tap_index[:, :, None] == jnp.arange(TAPS, dtype=jnp.int32)[None, None, :]).astype(jnp.float32)
    return jnp.sum(one_hot * kernel_row[None, None, :], axis=2)


def blur_forward(volume, kernels):
    along_x = band_matrix(kernels[0], NX, NX, 0, 1)
    along_y = band_matrix(kernels[1], NY, NY, 0, 1)
    volume = jnp.einsum("zxy,ox->zoy", volume, along_x, precision=lax.Precision.HIGHEST)
    volume = jnp.einsum("zxy,oy->zxo", volume, along_y, precision=lax.Precision.HIGHEST)
    padded = jnp.pad(volume, ((RADIUS, RADIUS), (0, 0), (0, 0)))
    result = jnp.zeros_like(volume)
    for tap in range(TAPS):
        result = result + kernels[2, tap] * padded[tap:tap + NZ]
    return result


def blur_adjoint(volume, kernels):
    padded = jnp.pad(volume, ((RADIUS, RADIUS), (0, 0), (0, 0)))
    result = jnp.zeros_like(volume)
    for tap in range(TAPS):
        begin = 2 * RADIUS - tap
        result = result + kernels[2, tap] * padded[begin:begin + NZ]
    along_y = band_matrix(kernels[1], NY, NY, 0, -1)
    along_x = band_matrix(kernels[0], NX, NX, 0, -1)
    result = jnp.einsum("zxy,oy->zxo", result, along_y, precision=lax.Precision.HIGHEST)
    return jnp.einsum("zxy,ox->zoy", result, along_x, precision=lax.Precision.HIGHEST)


def reference(views_data, psf, start):
    estimate = start
    for iteration in range(ITERS):
        log_sum = jnp.zeros_like(estimate)
        for view_index in range(VIEWS):
            kernels = psf[view_index] / jnp.sum(psf[view_index], axis=1, keepdims=True)
            blurred = blur_forward(estimate, kernels)
            quotient = views_data[view_index].astype(jnp.float32) / blurred
            correction = blur_adjoint(quotient, kernels)
            log_sum = log_sum + jnp.log(correction)
        estimate = estimate * jnp.exp(log_sum / VIEWS)
    return estimate
```

```python
import jax
import jax.numpy as jnp
from jax import lax
from jax.sharding import PartitionSpec as P

RADIUS = 15
TAPS = 31
ITERS = 2
PREC = lax.Precision.HIGH


def halo_planes(block):
    count = lax.axis_size("gz")
    forward = [(i, i + 1) for i in range(count - 1)]
    backward = [(target, source) for source, target in forward]
    low = lax.ppermute(block[block.shape[0] - RADIUS:], "gz", forward)
    high = lax.ppermute(block[:RADIUS], "gz", backward)
    return low, high


def band(kernel_row, out_pos, in_pos, direction):
    tap_index = direction * (in_pos[None, :] - out_pos[:, None]) + RADIUS
    one_hot = (tap_index[:, :, None] == jnp.arange(TAPS, dtype=jnp.int32)[None, None, :]).astype(
        jnp.float32
    )
    return jnp.sum(one_hot * kernel_row[None, None, :], axis=2)


def partner(piece, k):
    count = lax.axis_size("view")
    return lax.ppermute(piece, "view", [(i, i ^ k) for i in range(count)])


def blur_x(volume, matrix):
    return jnp.einsum("zxy,ox->zoy", volume, matrix, precision=PREC)


def blur_y(volume, matrix):
    return jnp.einsum("zxy,oy->zxo", volume, matrix, precision=PREC)


def blur_z(volume, matrix):
    return jnp.einsum("zxy,oz->oxy", volume, matrix, precision=PREC)


def per_device(views_data, psf, start):
    kernels = psf[0] / jnp.sum(psf[0], axis=1, keepdims=True)
    recorded = views_data[0]
    depth, nx, ny = recorded.shape
    views = lax.axis_size("view")
    v = lax.axis_index("view")
    rows = nx // views

    natural_x = jnp.arange(nx, dtype=jnp.int32)
    swapped_x = ((natural_x // rows) ^ v) * rows + natural_x % rows
    natural_y = jnp.arange(ny, dtype=jnp.int32)
    own_z = jnp.arange(depth, dtype=jnp.int32)
    wide_z = jnp.concatenate(
        [own_z, jnp.arange(RADIUS, dtype=jnp.int32) - RADIUS, jnp.arange(RADIUS, dtype=jnp.int32) + depth]
    )
    forward_x = [band(kernels[0], natural_x, natural_x, 1), band(kernels[0], natural_x, swapped_x, 1)]
    forward_y = band(kernels[1], natural_y, natural_y, 1)
    forward_z = band(kernels[2], own_z, wide_z, 1)
    adjoint_x = band(kernels[0], swapped_x, natural_x, -1)
    adjoint_y = band(kernels[1], natural_y, natural_y, -1)
    adjoint_z = band(kernels[2], own_z, wide_z, -1)

    own_piece = lax.dynamic_slice_in_dim(start, v * rows, rows, axis=1)
    blur_input = start
    for iteration in range(ITERS):
        low, high = halo_planes(blur_input.astype(jnp.bfloat16))
        wide = jnp.concatenate([blur_input, low.astype(blur_input.dtype), high.astype(blur_input.dtype)], axis=0)
        blurred = blur_y(blur_x(blur_z(wide.astype(jnp.float32), forward_z), forward_x[min(iteration, 1)]), forward_y)
        quotient = recorded.astype(jnp.float32) / blurred
        low, high = halo_planes(quotient.astype(jnp.bfloat16))
        wide = jnp.concatenate([quotient, low.astype(jnp.float32), high.astype(jnp.float32)], axis=0)
        correction = blur_y(blur_x(blur_z(wide, adjoint_z), adjoint_x), adjoint_y)
        log_term = jnp.log(correction)
        pieces = [log_term[:, k * rows:(k + 1) * rows] for k in range(views)]
        log_sum = pieces[0]
        for k in range(1, views):
            log_sum = log_sum + partner(pieces[k].astype(jnp.float16), k).astype(jnp.float32)
        own_piece = own_piece * jnp.exp(log_sum / views)
        if iteration < ITERS - 1:
            wire = own_piece.astype(jnp.bfloat16)
            blur_input = jnp.concatenate([wire] + [partner(wire, k) for k in range(1, views)], axis=1)
    top = jnp.max(own_piece, axis=(1, 2))
    exponent = jnp.maximum(jnp.ceil(jnp.log2(top)), -100.0)
    scaled = own_piece * jnp.exp2(15.0 - exponent)[:, None, None]
    note = jnp.broadcast_to(exponent.reshape(depth // rows, rows, 1), (depth // rows, rows, ny))
    wire = jnp.concatenate([scaled, note], axis=0).astype(jnp.float16)
    estimate = jnp.zeros((depth, nx, ny), jnp.float32)
    estimate = lax.dynamic_update_slice(estimate, own_piece, (0, v * rows, 0))
    for k in range(1, views):
        got = partner(wire, k).astype(jnp.float32)
        scale = jnp.exp2(got[depth:, :, 0].reshape(depth) - 15.0)
        estimate = lax.dynamic_update_slice(
            estimate, got[:depth] * scale[:, None, None], (0, (v ^ k) * rows, 0)
        )
    return estimate


def solution(mesh):
    in_specs = (P("view", "gz", None, None), P("view", None, None), P("gz", None, None))
    out_specs = P("gz", None, None)
    return jax.shard_map(
        per_device, mesh=mesh, in_specs=in_specs, out_specs=out_specs, check_vma=False
    )
```

```python
import jax
import jax.numpy as jnp
import numpy as np
from jax import lax
from jax.experimental import pallas as pl
from jax.experimental.pallas import tpu as pltpu
from jax.sharding import PartitionSpec as P

RADIUS = 15
TAPS = 31
ITERS = 2
F32, BF16 = jnp.float32, jnp.bfloat16
GROUP = 8

_PHASE = np.arange(16)[:, None] * 0.7548776662 + np.arange(256)[None, :] * 0.5698402909
SPREAD = (1.0 + _PHASE % 1.0).astype(np.float32)
UNSPREAD = (1.0 / SPREAD.astype(np.float64)).astype(np.float32)


def call(kernel, outs, args, scratch=(), smem=0):
    specs = [pl.BlockSpec(memory_space=pltpu.SMEM)] * smem
    specs += [pl.BlockSpec(memory_space=pltpu.VMEM)] * (len(args) - smem)
    return pl.pallas_call(
        kernel,
        out_shape=[jax.ShapeDtypeStruct(shape, dtype) for shape, dtype in outs],
        in_specs=specs,
        out_specs=[pl.BlockSpec(memory_space=pltpu.VMEM)] * len(outs),
        scratch_shapes=list(scratch),
        compiler_params=pltpu.CompilerParams(vmem_limit_bytes=40 * 1024 * 1024),
        cost_estimate=pl.CostEstimate(flops=1000, bytes_accessed=1000, transcendentals=0),
    )(*args)


def split(a):
    high = a.astype(BF16)
    return high, (a - high.astype(F32)).astype(BF16)


def mul(a, b):
    return jnp.dot(a, b, preferred_element_type=F32)


def mul3(a, b):
    return mul(a[0], b[0]) + mul(a[0], b[1]) + mul(a[1], b[0])


def tile_rows(pattern, rows):
    return jnp.concatenate([pattern] * (rows // pattern.shape[0]), axis=0)


def band_kernel(n_near, n_far, core_ref, taps_ref, *outs):
    depth = n_near + n_far
    core = core_ref[0]
    near_at, far_at = (depth - n_near) * core, (depth - n_far) * (1 - core)
    natural = lambda i: i
    ordered = lambda i: jnp.where(i < n_far, far_at + i, near_at + i - n_far)
    near = lambda i: near_at + i
    ext = lambda i: i + jnp.where(core == 0, -n_near, depth)
    sib = lambda i: i + jnp.where(core == 0, depth, -n_far)
    plans = [
        (0, natural, natural, 1, 1), (0, natural, natural, -1, 1),
        (1, natural, natural, -1, 1), (1, natural, natural, 1, 1),
        (2, ordered, natural, 1, GROUP), (2, ordered, sib, 1, GROUP), (2, near, ext, 1, GROUP),
        (2, ordered, ordered, -1, GROUP), (2, ordered, sib, -1, GROUP), (2, near, ext, -1, GROUP),
    ]
    for out, (axis, out_pos, in_pos, direction, repeat) in zip(outs, plans):
        row = lax.broadcasted_iota(jnp.int32, out.shape, 0)
        column = lax.broadcasted_iota(jnp.int32, out.shape, 1)
        tap = direction * (in_pos(column // repeat) - out_pos(row // repeat)) + RADIUS
        if repeat > 1:
            tap = jnp.where(row % repeat == column % repeat, tap, -1)
        total = jnp.zeros(out.shape, F32)
        for k in range(TAPS):
            total = total + jnp.where(tap == k, taps_ref[axis, k], 0.0)
        out[...] = total


def blur_rows(planes, mx, my):
    return mul3(split(mul3(mx, split(planes))), my)


def z_rows(own, sib_ref, at, half, wo, ws, unspread):
    n_sib = sib_ref.shape[0]
    total = mul3(wo, split(own))
    sib = sib_ref[:, pl.ds(at, 16), :].astype(F32)[:, half * GROUP:(half + 1) * GROUP]
    sib = jnp.concatenate(
        [sib.reshape(n_sib * GROUP, -1), jnp.zeros((ws[0].shape[1] - n_sib * GROUP, sib.shape[2]), F32)], axis=0
    ).astype(BF16)
    other = mul(ws[0], sib) + mul(ws[1], sib)
    scale = unspread[half * GROUP:(half + 1) * GROUP]
    return total + other * tile_rows(scale, other.shape[0])


def fill_z(own_refs, sib_ref, wo_ref, ws_ref, unspread_ref, far_ref, near_ref):
    wo, ws, unspread = split(wo_ref[...]), split(ws_ref[...]), unspread_ref[...]
    nx, ny = far_ref.shape[1:]

    def step(g, _):
        at = pl.multiple_of(g * 16, 16)
        for half in range(2):
            here = pl.ds(pl.multiple_of(at + half * GROUP, GROUP), GROUP)
            own = jnp.concatenate([r[:, here, :].reshape(r.shape[0] * GROUP, ny) for r in own_refs], axis=0)
            out = z_rows(own, sib_ref, at, half, wo, ws, unspread)
            cut = far_ref.shape[0] * GROUP
            far_ref[:, here, :] = out[:cut].reshape(far_ref.shape[0], GROUP, ny)
            near_ref[:, here, :] = out[cut:].reshape(near_ref.shape[0], GROUP, ny)
        return 0

    lax.fori_loop(0, nx // 16, step, 0)


def add_ext(ext_ref, we_ref, unspread_ref, near_ref, out_ref):
    we, unspread = split(we_ref[...]), unspread_ref[...]
    n, nx, ny = near_ref.shape

    def step(g, _):
        at = pl.multiple_of(g * 16, 16)
        block = ext_ref[:, pl.ds(at, 16), :].astype(F32)
        for half in range(2):
            here = pl.ds(pl.multiple_of(at + half * GROUP, GROUP), GROUP)
            ext = block[:, half * GROUP:(half + 1) * GROUP].reshape(n * GROUP, ny)
            ext = jnp.concatenate([ext, jnp.zeros((we[0].shape[1] - n * GROUP, ny), F32)], axis=0).astype(BF16)
            other = (mul(we[0], ext) + mul(we[1], ext))[:n * GROUP]
            other = other * tile_rows(unspread[half * GROUP:(half + 1) * GROUP], n * GROUP)
            out_ref[:, here, :] = near_ref[:, here, :] + other.reshape(n, GROUP, ny)
        return 0

    lax.fori_loop(0, nx // 16, step, 0)


def to_quotient(load, count, recorded_ref, mx_ref, my_ref, spread_ref, quotient_ref, wire_ref):
    mx, my = split(mx_ref[...]), split(my_ref[...])
    pattern = tile_rows(spread_ref[...], recorded_ref.shape[1])

    def step(p, _):
        quotient = recorded_ref[p].astype(F32) / blur_rows(load(p), mx, my)
        quotient_ref[p] = quotient
        wire_ref[p] = (quotient * pattern).astype(BF16)
        return 0

    lax.fori_loop(0, count, step, 0)


def to_log(load, count, mx_ref, my_ref, log_ref):
    mx, my = split(mx_ref[...]), split(my_ref[...])
    views, _, rows, ny = log_ref.shape

    def step(p, _):
        log_ref[:, p] = jnp.log(blur_rows(load(p), mx, my)).reshape(views, rows, ny)
        return 0

    lax.fori_loop(0, count, step, 0)


def first_far_kernel(start_ref, sib_ref, wo_ref, ws_ref, unspread_ref, recorded_ref, mx_ref, my_ref, spread_ref,
                     quotient_ref, wire_ref, near_ref, far_ref):
    fill_z([start_ref], sib_ref, wo_ref, ws_ref, unspread_ref, far_ref, near_ref)
    to_quotient(lambda p: far_ref[p], quotient_ref.shape[0], recorded_ref, mx_ref, my_ref, spread_ref, quotient_ref, wire_ref)


def first_near_kernel(near_ref, ext_ref, we_ref, unspread_ref, recorded_ref, mx_ref, my_ref, spread_ref,
                      quotient_ref, wire_ref, sum_ref):
    add_ext(ext_ref, we_ref, unspread_ref, near_ref, sum_ref)
    to_quotient(lambda p: sum_ref[p], quotient_ref.shape[0], recorded_ref, mx_ref, my_ref, spread_ref, quotient_ref, wire_ref)


def block_kernel(first, blocks_ref, unspread_ref, recorded_ref, mx_ref, my_ref, spread_ref, quotient_ref, wire_ref):
    views, _, rows, ny = blocks_ref.shape
    pattern = tile_rows(unspread_ref[...], views * rows)

    def load(p):
        return blocks_ref[:, first + p].reshape(views * rows, ny).astype(F32) * pattern

    to_quotient(load, quotient_ref.shape[0], recorded_ref, mx_ref, my_ref, spread_ref, quotient_ref, wire_ref)


def adjoint_far_kernel(far_q_ref, near_q_ref, sib_ref, wo_ref, ws_ref, unspread_ref, mx_ref, my_ref, log_ref, near_ref, far_ref):
    fill_z([far_q_ref, near_q_ref], sib_ref, wo_ref, ws_ref, unspread_ref, far_ref, near_ref)
    to_log(lambda p: far_ref[p], far_ref.shape[0], mx_ref, my_ref, log_ref)


def adjoint_near_kernel(near_ref, ext_ref, _, we_ref, unspread_ref, mx_ref, my_ref, log_ref, sum_ref):
    add_ext(ext_ref, we_ref, unspread_ref, near_ref, sum_ref)
    to_log(lambda p: sum_ref[p], sum_ref.shape[0], mx_ref, my_ref, log_ref)


def assemble_kernel(blocks_ref, out_ref):
    depth, rows, ny = out_ref.shape
    for z in range(depth):
        exponent = blocks_ref[0, depth + z // rows, z % rows:z % rows + 1, :]
        out_ref[z] = blocks_ref[0, z] * jnp.exp2(exponent - 15.0)


def assemble(blocks, depth):
    views, planes, rows, ny = blocks.shape
    return pl.pallas_call(
        assemble_kernel,
        grid=(views,),
        out_shape=jax.ShapeDtypeStruct((depth, views * rows, ny), F32),
        in_specs=[pl.BlockSpec((1, planes, rows, ny), lambda j: (j, 0, 0, 0))],
        out_specs=pl.BlockSpec((depth, rows, ny), lambda j: (0, j, 0)),
        compiler_params=pltpu.CompilerParams(vmem_limit_bytes=20 * 1024 * 1024),
        cost_estimate=pl.CostEstimate(flops=1000, bytes_accessed=1000, transcendentals=0),
    )(blocks)


def to_other_chip(planes):
    count = lax.axis_size("gz")
    pairs = [(i, i + 1) for i in range(1, count - 1, 2)]
    return lax.ppermute(planes, "gz", pairs + [(b, a) for a, b in pairs])


def to_sibling(planes):
    count = lax.axis_size("gz")
    return lax.ppermute(planes, "gz", [(i, i ^ 1) for i in range(count)])


def to_views(blocks):
    return lax.all_to_all(blocks, "view", 0, 0)


def sum_over_views(log_blocks):
    return jnp.sum(to_views(log_blocks.astype(jnp.float16)).astype(F32), axis=0)


def band(kernel_row, out_pos, in_pos):
    tap_index = in_pos[None, :] - out_pos[:, None] + RADIUS
    one_hot = (tap_index[:, :, None] == jnp.arange(TAPS, dtype=jnp.int32)[None, None, :]).astype(F32)
    return jnp.sum(one_hot * kernel_row[None, None, :], axis=2)


def gather_result(piece):
    views = lax.axis_size("view")
    depth, rows, ny = piece.shape
    extra = -(-depth // rows)
    exponent = jnp.maximum(jnp.ceil(jnp.log2(jnp.max(piece, axis=(1, 2)))), -100.0)
    scaled = piece * jnp.exp2(15.0 - exponent)[:, None, None]
    note = jnp.pad(exponent, (0, extra * rows - depth)).reshape(extra, rows, 1)
    note = jnp.broadcast_to(note, (extra, rows, ny))
    wire = jnp.concatenate([scaled, note], axis=0).astype(jnp.float16)
    return assemble(to_views(jnp.broadcast_to(wire[None], (views,) + wire.shape)).astype(F32), depth)


def per_device(views_data, psf, start):
    kernels = psf[0] / jnp.sum(psf[0], axis=1, keepdims=True)
    recorded = views_data[0]
    depth, nx, ny = recorded.shape
    views = lax.axis_size("view")
    v = lax.axis_index("view")
    core = lax.axis_index("gz") % 2
    rows = nx // views
    n_near, n_far = RADIUS, depth - RADIUS
    spread, unspread = jnp.asarray(SPREAD), jnp.asarray(UNSPREAD)

    near_at, far_at = (depth - n_near) * core, (depth - n_far) * (1 - core)

    def near_of(a):
        return lax.dynamic_slice_in_dim(a, near_at, n_near, axis=0)

    def far_of(a):
        return lax.dynamic_slice_in_dim(a, far_at, n_far, axis=0)

    def to_wire(planes):
        count = planes.shape[-2] // spread.shape[0]
        return (planes * jnp.concatenate([spread] * count, axis=0)).astype(BF16)

    ext = to_other_chip(to_wire(near_of(start)))
    sib = to_sibling(to_wire(far_of(start)))

    full, wide, small = depth * GROUP, 256, 128
    near_rows = n_near * GROUP
    matrices = call(
        lambda *refs: band_kernel(n_near, n_far, *refs),
        [((nx, nx), F32)] * 2 + [((ny, ny), F32)] * 2
        + [((full, full), F32), ((full, 144), F32), ((near_rows, small), F32)] * 2,
        [core.reshape(1).astype(jnp.int32), kernels],
        smem=2,
    )
    forward_x, adjoint_x, forward_y, adjoint_y, forward_o, forward_s, forward_e, adjoint_o, adjoint_s, adjoint_e = matrices

    own_rows = lax.dynamic_slice_in_dim(start, v * rows, rows, axis=1)
    piece_far, piece_near = far_of(own_rows), near_of(own_rows)
    recorded_far, recorded_near = far_of(recorded), near_of(recorded)

    count = jnp.arange(depth, dtype=jnp.int32)
    out_z = jnp.where(count < n_far, far_at + count, near_at + count - n_far)
    sib_z = count[:n_far] + jnp.where(core == 0, depth, -n_far)
    ext_z = count[:n_near] + jnp.where(core == 0, -n_near, depth)
    wide_z = jnp.concatenate([out_z, sib_z, ext_z])
    every_z = jnp.broadcast_to(jnp.pad(kernels[2], (0, 128 - TAPS)), (views, GROUP, 128))
    every_z = to_views(every_z)[:, 0, :TAPS]
    forward_all = jax.vmap(lambda kernel_row: band(kernel_row, out_z, wide_z))(every_z)

    far_shape, near_shape = (n_far, nx, ny), (n_near, nx, ny)
    quotient_far, wire_far, partly = call(
        first_far_kernel,
        [(far_shape, F32), (far_shape, BF16), (near_shape, F32)],
        [start, sib, forward_o, forward_s, unspread, recorded_far, forward_x, forward_y, spread],
        [pltpu.VMEM(far_shape, F32)],
    )
    sib = to_sibling(wire_far)
    quotient_near, wire_near = call(
        first_near_kernel,
        [(near_shape, F32), (near_shape, BF16)],
        [partly, ext, forward_e, unspread, recorded_near, forward_x, forward_y, spread],
        [pltpu.VMEM(near_shape, F32)],
    )
    ext = to_other_chip(wire_near)

    for iteration in range(ITERS):
        log_far, partly = call(
            adjoint_far_kernel,
            [((views, n_far, rows, ny), F32), (near_shape, F32)],
            [quotient_far, quotient_near, sib, adjoint_o, adjoint_s, unspread, adjoint_x, adjoint_y],
            [pltpu.VMEM(far_shape, F32)],
        )
        sum_far = sum_over_views(log_far)
        piece_far = piece_far * jnp.exp(sum_far / views)

        (log_near,) = call(
            adjoint_near_kernel,
            [((views, n_near, rows, ny), F32)],
            [partly, ext, sum_far[0, :8], adjoint_e, unspread, adjoint_x, adjoint_y],
            [pltpu.VMEM(near_shape, F32)],
        )
        piece_near = piece_near * jnp.exp(sum_over_views(log_near) / views)

        if iteration < ITERS - 1:
            ext = to_other_chip(to_wire(piece_near))
            sib = to_sibling(to_wire(piece_far))
            planes = jnp.concatenate(
                [piece_far, piece_near, sib.astype(F32) * unspread, ext.astype(F32) * unspread], axis=0
            )
            blocks = jnp.einsum("zxy,voz->voxy", planes, forward_all, precision=lax.Precision.HIGH)
            blocks = to_views(to_wire(blocks))
            quotient_near, wire_near = call(
                lambda *refs: block_kernel(n_far, *refs),
                [(near_shape, F32), (near_shape, BF16)],
                [blocks, unspread, recorded_near, forward_x, forward_y, spread],
            )
            ext = to_other_chip(wire_near)
            quotient_far, wire_far = call(
                lambda *refs: block_kernel(0, *refs),
                [(far_shape, F32), (far_shape, BF16)],
                [blocks, unspread, recorded_far, forward_x, forward_y, spread],
            )
            sib = to_sibling(wire_far)

    both = jnp.concatenate([piece_near, piece_far, piece_near], axis=0)
    return gather_result(lax.dynamic_slice_in_dim(both, n_near * core, depth, axis=0))


def solution(mesh):
    in_specs = (P("view", "gz", None, None), P("view", None, None), P("gz", None, None))
    out_specs = P("gz", None, None)
    return jax.shard_map(
        per_device, mesh=mesh, in_specs=in_specs, out_specs=out_specs, check_vma=False
    )
```

```python
import jax
import jax.numpy as jnp
import numpy as np
from jax import lax
from jax.experimental import pallas as pl
from jax.experimental.pallas import tpu as pltpu
from jax.sharding import PartitionSpec as P

RADIUS = 15
TAPS = 31
ITERS = 2
F32, BF16 = jnp.float32, jnp.bfloat16
GROUP = 8

_PHASE = np.arange(16)[:, None] * 0.7548776662 + np.arange(256)[None, :] * 0.5698402909
SPREAD = (1.0 + _PHASE % 1.0).astype(np.float32)
UNSPREAD = (1.0 / SPREAD.astype(np.float64)).astype(np.float32)


LIGHT = pl.CostEstimate(flops=1000, bytes_accessed=1000, transcendentals=0)
HEAVY = pl.CostEstimate(flops=6 * 10**10, bytes_accessed=2 * 10**8, transcendentals=0)


def call(kernel, outs, args, scratch=(), smem=0, cost=LIGHT):
    specs = [pl.BlockSpec(memory_space=pltpu.SMEM)] * smem
    specs += [pl.BlockSpec(memory_space=pltpu.VMEM)] * (len(args) - smem)
    return pl.pallas_call(
        kernel,
        out_shape=[jax.ShapeDtypeStruct(shape, dtype) for shape, dtype in outs],
        in_specs=specs,
        out_specs=[pl.BlockSpec(memory_space=pltpu.VMEM)] * len(outs),
        scratch_shapes=list(scratch),
        compiler_params=pltpu.CompilerParams(vmem_limit_bytes=40 * 1024 * 1024),
        cost_estimate=cost,
    )(*args)


def split(a):
    high = a.astype(BF16)
    return high, (a - high.astype(F32)).astype(BF16)


def mul(a, b):
    return jnp.dot(a, b, preferred_element_type=F32)


def mul3(a, b):
    return mul(a[0], b[0]) + mul(a[0], b[1]) + mul(a[1], b[0])


def tile_rows(pattern, rows):
    return jnp.concatenate([pattern] * (rows // pattern.shape[0]), axis=0)


def band_kernel(n_near, n_far, core_ref, taps_ref, *outs):
    depth = n_near + n_far
    core = core_ref[0]
    near_at, far_at = (depth - n_near) * core, (depth - n_far) * (1 - core)
    natural = lambda i: i
    ordered = lambda i: jnp.where(i < n_far, far_at + i, near_at + i - n_far)
    near = lambda i: near_at + i
    ext = lambda i: i + jnp.where(core == 0, -n_near, depth)
    sib = lambda i: i + jnp.where(core == 0, depth, -n_far)
    plans = [
        (0, natural, natural, 1, 1), (0, natural, natural, -1, 1),
        (1, natural, natural, -1, 1), (1, natural, natural, 1, 1),
        (2, ordered, natural, 1, GROUP), (2, ordered, sib, 1, GROUP), (2, near, ext, 1, GROUP),
        (2, ordered, ordered, -1, GROUP), (2, ordered, sib, -1, GROUP), (2, near, ext, -1, GROUP),
    ]
    for out, (axis, out_pos, in_pos, direction, repeat) in zip(outs, plans):
        row = lax.broadcasted_iota(jnp.int32, out.shape, 0)
        column = lax.broadcasted_iota(jnp.int32, out.shape, 1)
        tap = direction * (in_pos(column // repeat) - out_pos(row // repeat)) + RADIUS
        if repeat > 1:
            tap = jnp.where(row % repeat == column % repeat, tap, -1)
        total = jnp.zeros(out.shape, F32)
        for k in range(TAPS):
            total = total + jnp.where(tap == k, taps_ref[axis, k], 0.0)
        out[...] = total


def blur_rows(planes, mx, my):
    return mul3(split(mul3(mx, split(planes))), my)


def z_rows(own, sib_ref, at, half, wo, ws, unspread):
    n_sib = sib_ref.shape[0]
    total = mul3(wo, split(own))
    sib = sib_ref[:, pl.ds(at, 16), :].astype(F32)[:, half * GROUP:(half + 1) * GROUP]
    sib = jnp.concatenate(
        [sib.reshape(n_sib * GROUP, -1), jnp.zeros((ws[0].shape[1] - n_sib * GROUP, sib.shape[2]), F32)], axis=0
    ).astype(BF16)
    other = mul(ws[0], sib) + mul(ws[1], sib)
    scale = unspread[half * GROUP:(half + 1) * GROUP]
    return total + other * tile_rows(scale, other.shape[0])


def fill_z(own_refs, sib_ref, wo_ref, ws_ref, unspread_ref, far_ref, near_ref):
    wo, ws, unspread = split(wo_ref[...]), split(ws_ref[...]), unspread_ref[...]
    nx, ny = far_ref.shape[1:]

    def step(g, _):
        at = pl.multiple_of(g * 16, 16)
        for half in range(2):
            here = pl.ds(pl.multiple_of(at + half * GROUP, GROUP), GROUP)
            own = jnp.concatenate([r[:, here, :].reshape(r.shape[0] * GROUP, ny) for r in own_refs], axis=0)
            out = z_rows(own, sib_ref, at, half, wo, ws, unspread)
            cut = far_ref.shape[0] * GROUP
            far_ref[:, here, :] = out[:cut].reshape(far_ref.shape[0], GROUP, ny)
            near_ref[:, here, :] = out[cut:].reshape(near_ref.shape[0], GROUP, ny)
        return 0

    lax.fori_loop(0, nx // 16, step, 0)


def add_ext(ext_ref, we_ref, unspread_ref, near_ref, out_ref):
    we, unspread = split(we_ref[...]), unspread_ref[...]
    n, nx, ny = near_ref.shape

    def step(g, _):
        at = pl.multiple_of(g * 16, 16)
        block = ext_ref[:, pl.ds(at, 16), :].astype(F32)
        for half in range(2):
            here = pl.ds(pl.multiple_of(at + half * GROUP, GROUP), GROUP)
            ext = block[:, half * GROUP:(half + 1) * GROUP].reshape(n * GROUP, ny)
            ext = jnp.concatenate([ext, jnp.zeros((we[0].shape[1] - n * GROUP, ny), F32)], axis=0).astype(BF16)
            other = (mul(we[0], ext) + mul(we[1], ext))[:n * GROUP]
            other = other * tile_rows(unspread[half * GROUP:(half + 1) * GROUP], n * GROUP)
            out_ref[:, here, :] = near_ref[:, here, :] + other.reshape(n, GROUP, ny)
        return 0

    lax.fori_loop(0, nx // 16, step, 0)


def to_quotient(load, count, recorded_ref, mx_ref, my_ref, spread_ref, quotient_ref, wire_ref):
    mx, my = split(mx_ref[...]), split(my_ref[...])
    pattern = tile_rows(spread_ref[...], recorded_ref.shape[1])

    for p in range(count):
        quotient = recorded_ref[p].astype(F32) / blur_rows(load(p), mx, my)
        quotient_ref[p] = quotient
        wire_ref[p] = (quotient * pattern).astype(BF16)


def to_log(load, count, mx_ref, my_ref, log_ref):
    mx, my = split(mx_ref[...]), split(my_ref[...])
    views, _, rows, ny = log_ref.shape

    for p in range(count):
        log_ref[:, p] = jnp.log(blur_rows(load(p), mx, my)).reshape(views, rows, ny)


def first_far_kernel(start_ref, sib_ref, wo_ref, ws_ref, unspread_ref, recorded_ref, mx_ref, my_ref, spread_ref,
                     quotient_ref, wire_ref, near_ref, far_ref):
    fill_z([start_ref], sib_ref, wo_ref, ws_ref, unspread_ref, far_ref, near_ref)
    to_quotient(lambda p: far_ref[p], quotient_ref.shape[0], recorded_ref, mx_ref, my_ref, spread_ref, quotient_ref, wire_ref)


def first_near_kernel(near_ref, ext_ref, we_ref, unspread_ref, recorded_ref, mx_ref, my_ref, spread_ref,
                      quotient_ref, wire_ref, sum_ref):
    add_ext(ext_ref, we_ref, unspread_ref, near_ref, sum_ref)
    to_quotient(lambda p: sum_ref[p], quotient_ref.shape[0], recorded_ref, mx_ref, my_ref, spread_ref, quotient_ref, wire_ref)


def block_kernel(first, blocks_ref, unspread_ref, recorded_ref, mx_ref, my_ref, spread_ref, quotient_ref, wire_ref):
    views, _, rows, ny = blocks_ref.shape
    pattern = tile_rows(unspread_ref[...], views * rows)

    def load(p):
        return blocks_ref[:, first + p].reshape(views * rows, ny).astype(F32) * pattern

    to_quotient(load, quotient_ref.shape[0], recorded_ref, mx_ref, my_ref, spread_ref, quotient_ref, wire_ref)


def adjoint_far_kernel(far_q_ref, near_q_ref, sib_ref, wo_ref, ws_ref, unspread_ref, mx_ref, my_ref, log_ref, near_ref, far_ref):
    fill_z([far_q_ref, near_q_ref], sib_ref, wo_ref, ws_ref, unspread_ref, far_ref, near_ref)
    to_log(lambda p: far_ref[p], far_ref.shape[0], mx_ref, my_ref, log_ref)


def adjoint_near_kernel(near_ref, ext_ref, we_ref, unspread_ref, mx_ref, my_ref, log_ref, sum_ref):
    add_ext(ext_ref, we_ref, unspread_ref, near_ref, sum_ref)
    to_log(lambda p: sum_ref[p], sum_ref.shape[0], mx_ref, my_ref, log_ref)


def assemble_kernel(blocks_ref, out_ref):
    depth, rows, ny = out_ref.shape
    for z in range(depth):
        exponent = blocks_ref[0, depth + z // rows, z % rows:z % rows + 1, :]
        out_ref[z] = blocks_ref[0, z] * jnp.exp2(exponent - 15.0)


def assemble(blocks, depth):
    views, planes, rows, ny = blocks.shape
    return pl.pallas_call(
        assemble_kernel,
        grid=(views,),
        out_shape=jax.ShapeDtypeStruct((depth, views * rows, ny), F32),
        in_specs=[pl.BlockSpec((1, planes, rows, ny), lambda j: (j, 0, 0, 0))],
        out_specs=pl.BlockSpec((depth, rows, ny), lambda j: (0, j, 0)),
        compiler_params=pltpu.CompilerParams(vmem_limit_bytes=20 * 1024 * 1024),
        cost_estimate=LIGHT,
    )(blocks)


def to_other_chip(planes):
    count = lax.axis_size("gz")
    pairs = [(i, i + 1) for i in range(1, count - 1, 2)]
    return lax.ppermute(planes, "gz", pairs + [(b, a) for a, b in pairs])


def to_sibling(planes):
    count = lax.axis_size("gz")
    return lax.ppermute(planes, "gz", [(i, i ^ 1) for i in range(count)])


def to_views(blocks):
    return lax.all_to_all(blocks, "view", 0, 0)


def sum_over_views(log_blocks):
    return jnp.sum(to_views(log_blocks).astype(F32), axis=0)


def band(kernel_row, out_pos, in_pos):
    tap_index = in_pos[None, :] - out_pos[:, None] + RADIUS
    one_hot = (tap_index[:, :, None] == jnp.arange(TAPS, dtype=jnp.int32)[None, None, :]).astype(F32)
    return jnp.sum(one_hot * kernel_row[None, None, :], axis=2)


def gather_result(piece):
    views = lax.axis_size("view")
    depth, rows, ny = piece.shape
    extra = -(-depth // rows)
    exponent = jnp.maximum(jnp.ceil(jnp.log2(jnp.max(piece, axis=(1, 2)))), -100.0)
    scaled = piece * jnp.exp2(15.0 - exponent)[:, None, None]
    note = jnp.pad(exponent, (0, extra * rows - depth)).reshape(extra, rows, 1)
    note = jnp.broadcast_to(note, (extra, rows, ny))
    wire = jnp.concatenate([scaled, note], axis=0).astype(jnp.float16)
    return assemble(to_views(jnp.broadcast_to(wire[None], (views,) + wire.shape)).astype(F32), depth)


def per_device(views_data, psf, start):
    kernels = psf[0] / jnp.sum(psf[0], axis=1, keepdims=True)
    recorded = views_data[0]
    depth, nx, ny = recorded.shape
    views = lax.axis_size("view")
    v = lax.axis_index("view")
    core = lax.axis_index("gz") % 2
    rows = nx // views
    n_near, n_far = RADIUS, depth - RADIUS
    spread, unspread = jnp.asarray(SPREAD), jnp.asarray(UNSPREAD)

    near_at, far_at = (depth - n_near) * core, (depth - n_far) * (1 - core)

    def near_of(a):
        return lax.dynamic_slice_in_dim(a, near_at, n_near, axis=0)

    def far_of(a):
        return lax.dynamic_slice_in_dim(a, far_at, n_far, axis=0)

    def to_wire(planes):
        count = planes.shape[-2] // spread.shape[0]
        return (planes * jnp.concatenate([spread] * count, axis=0)).astype(BF16)

    ext = to_other_chip(to_wire(near_of(start)))
    sib = to_sibling(to_wire(far_of(start)))

    full, wide, small = depth * GROUP, 256, 128
    near_rows = n_near * GROUP
    matrices = call(
        lambda *refs: band_kernel(n_near, n_far, *refs),
        [((nx, nx), F32)] * 2 + [((ny, ny), F32)] * 2
        + [((full, full), F32), ((full, 144), F32), ((near_rows, small), F32)] * 2,
        [core.reshape(1).astype(jnp.int32), kernels],
        smem=2,
    )
    forward_x, adjoint_x, forward_y, adjoint_y, forward_o, forward_s, forward_e, adjoint_o, adjoint_s, adjoint_e = matrices

    own_rows = lax.dynamic_slice_in_dim(start, v * rows, rows, axis=1)
    piece_far, piece_near = far_of(own_rows), near_of(own_rows)
    recorded_far, recorded_near = far_of(recorded), near_of(recorded)

    count = jnp.arange(depth, dtype=jnp.int32)
    out_z = jnp.where(count < n_far, far_at + count, near_at + count - n_far)
    sib_z = count[:n_far] + jnp.where(core == 0, depth, -n_far)
    ext_z = count[:n_near] + jnp.where(core == 0, -n_near, depth)
    wide_z = jnp.concatenate([out_z, sib_z, ext_z])
    every_z = jnp.broadcast_to(jnp.pad(kernels[2], (0, 128 - TAPS)), (views, GROUP, 128))
    every_z = to_views(every_z)[:, 0, :TAPS]
    forward_all = jax.vmap(lambda kernel_row: band(kernel_row, out_z, wide_z))(every_z)

    far_shape, near_shape = (n_far, nx, ny), (n_near, nx, ny)
    quotient_far, wire_far, partly = call(
        lambda _, *refs: first_far_kernel(*refs),
        [(far_shape, F32), (far_shape, BF16), (near_shape, F32)],
        [forward_all, start, sib, forward_o, forward_s, unspread, recorded_far, forward_x, forward_y, spread],
        [pltpu.VMEM(far_shape, F32)],
    )
    sib = to_sibling(wire_far)
    quotient_near, wire_near = call(
        first_near_kernel,
        [(near_shape, F32), (near_shape, BF16)],
        [partly, ext, forward_e, unspread, recorded_near, forward_x, forward_y, spread],
        [pltpu.VMEM(near_shape, F32)],
        cost=HEAVY,
    )
    ext = to_other_chip(wire_near)

    for iteration in range(ITERS):
        log_far, partly = call(
            adjoint_far_kernel,
            [((views, n_far, rows, ny), F32), (near_shape, F32)],
            [quotient_far, quotient_near, sib, adjoint_o, adjoint_s, unspread, adjoint_x, adjoint_y],
            [pltpu.VMEM(far_shape, F32)],
        )
        sum_far = sum_over_views(log_far.astype(jnp.float16))

        (log_near,) = call(
            adjoint_near_kernel,
            [((views, n_near, rows, ny), F32)],
            [partly, ext, adjoint_e, unspread, adjoint_x, adjoint_y],
            [pltpu.VMEM(near_shape, F32)],
            cost=HEAVY,
        )
        log_near, sum_far = lax.optimization_barrier((log_near.astype(jnp.float16), sum_far))
        piece_far = piece_far * jnp.exp(sum_far / views)
        piece_near = piece_near * jnp.exp(sum_over_views(log_near) / views)

        if iteration < ITERS - 1:
            ext = to_other_chip(to_wire(piece_near))
            sib = to_sibling(to_wire(piece_far))
            planes = jnp.concatenate(
                [piece_far, piece_near, sib.astype(F32) * unspread, ext.astype(F32) * unspread], axis=0
            )
            blocks = jnp.einsum("zxy,voz->voxy", planes, forward_all, precision=lax.Precision.HIGH)
            blocks = to_views(to_wire(blocks))
            quotient_near, wire_near = call(
                lambda *refs: block_kernel(n_far, *refs),
                [(near_shape, F32), (near_shape, BF16)],
                [blocks, unspread, recorded_near, forward_x, forward_y, spread],
                cost=HEAVY,
            )
            ext = to_other_chip(wire_near)
            quotient_far, wire_far = call(
                lambda _, *refs: block_kernel(0, *refs),
                [(far_shape, F32), (far_shape, BF16)],
                [wire_near, blocks, unspread, recorded_far, forward_x, forward_y, spread],
            )
            sib = to_sibling(wire_far)

    both = jnp.concatenate([piece_near, piece_far, piece_near], axis=0)
    return gather_result(lax.dynamic_slice_in_dim(both, n_near * core, depth, axis=0))


def solution(mesh):
    in_specs = (P("view", "gz", None, None), P("view", None, None), P("gz", None, None))
    out_specs = P("gz", None, None)
    return jax.shard_map(
        per_device, mesh=mesh, in_specs=in_specs, out_specs=out_specs, check_vma=False
    )
```

```python
import jax
import jax.numpy as jnp
import numpy as np
from jax import lax
from jax.experimental import pallas as pl
from jax.experimental.pallas import tpu as pltpu
from jax.sharding import PartitionSpec as P

RADIUS = 15
TAPS = 31
ITERS = 2
F32, BF16 = jnp.float32, jnp.bfloat16
GROUP = 8

_PHASE = np.arange(16)[:, None] * 0.7548776662 + np.arange(256)[None, :] * 0.5698402909
SPREAD = (1.0 + _PHASE % 1.0).astype(np.float32)
UNSPREAD = (1.0 / SPREAD.astype(np.float64)).astype(np.float32)


LIGHT = pl.CostEstimate(flops=1000, bytes_accessed=1000, transcendentals=0)
HEAVY = pl.CostEstimate(flops=6 * 10**10, bytes_accessed=2 * 10**8, transcendentals=0)


def call(kernel, outs, args, scratch=(), smem=0, far_off=(), unread=(), cost=LIGHT):
    specs = [pl.BlockSpec(memory_space=pltpu.SMEM)] * smem
    for i in range(smem, len(args)):
        space = pltpu.HBM if i in far_off else pl.ANY if i in unread else pltpu.VMEM
        specs.append(pl.BlockSpec(memory_space=space))
    return pl.pallas_call(
        kernel,
        out_shape=[jax.ShapeDtypeStruct(shape, dtype) for shape, dtype in outs],
        in_specs=specs,
        out_specs=[pl.BlockSpec(memory_space=pltpu.VMEM)] * len(outs),
        scratch_shapes=list(scratch),
        compiler_params=pltpu.CompilerParams(vmem_limit_bytes=16 * 1024 * 1024),
        cost_estimate=cost,
    )(*args)


def split(a):
    high = a.astype(BF16)
    return high, (a - high.astype(F32)).astype(BF16)


def mul(a, b):
    return jnp.dot(a, b, preferred_element_type=F32)


def mul3(a, b):
    return mul(a[0], b[0]) + mul(a[0], b[1]) + mul(a[1], b[0])


def tile_rows(pattern, rows):
    return jnp.concatenate([pattern] * (rows // pattern.shape[0]), axis=0)


X_FORWARD, X_ADJOINT = (0, 0, 128, 128), (0, 128, 128, 128)
Y_FORWARD, Y_ADJOINT = (128, 0, 256, 256), (384, 0, 256, 256)
OWN_FORWARD, OWN_ADJOINT = (640, 0, 256, 256), (896, 0, 256, 256)
SIB_FORWARD, SIB_ADJOINT = (1152, 0, 256, 144), (1408, 0, 256, 144)
EXT_FORWARD, EXT_ADJOINT = (1664, 0, 120, 128), (1664, 128, 120, 128)
MATRIX_ROWS = 1784


def matrix(ref, where):
    row, column, rows, columns = where
    return split(ref[row:row + rows, column:column + columns])


def band_kernel(n_near, n_far, core_ref, taps_ref, _, out_ref):
    depth = n_near + n_far
    core = core_ref[0]
    near_at, far_at = (depth - n_near) * core, (depth - n_far) * (1 - core)
    natural = lambda i: i
    ordered = lambda i: jnp.where(i < n_far, far_at + i, near_at + i - n_far)
    near = lambda i: near_at + i
    ext = lambda i: i + jnp.where(core == 0, -n_near, depth)
    sib = lambda i: jnp.where(i < n_far, i + jnp.where(core == 0, depth, -n_far), 4 * depth)
    plans = [
        (X_FORWARD, 0, natural, natural, 1, 1), (X_ADJOINT, 0, natural, natural, -1, 1),
        (Y_FORWARD, 1, natural, natural, -1, 1), (Y_ADJOINT, 1, natural, natural, 1, 1),
        (OWN_FORWARD, 2, ordered, natural, 1, GROUP), (OWN_ADJOINT, 2, ordered, ordered, -1, GROUP),
        (SIB_FORWARD, 2, ordered, sib, 1, GROUP), (SIB_ADJOINT, 2, ordered, sib, -1, GROUP),
        (EXT_FORWARD, 2, near, ext, 1, GROUP), (EXT_ADJOINT, 2, near, ext, -1, GROUP),
    ]
    for (at, column_at, rows, columns), axis, out_pos, in_pos, direction, repeat in plans:
        columns = -(-columns // 128) * 128
        row = lax.broadcasted_iota(jnp.int32, (rows, columns), 0)
        column = lax.broadcasted_iota(jnp.int32, (rows, columns), 1)
        tap = direction * (in_pos(column // repeat) - out_pos(row // repeat)) + RADIUS
        if repeat > 1:
            tap = jnp.where(row % repeat == column % repeat, tap, -1)
        total = jnp.zeros((rows, columns), F32)
        for k in range(TAPS):
            total = total + jnp.where(tap == k, taps_ref[axis, k], 0.0)
        out_ref[at:at + rows, column_at:column_at + columns] = total


def wire_kernel(at, count, core_ref, volume_ref, spread_ref, *refs):
    wire_ref, buffer, arrived = refs[-3:]
    first = jnp.where(core_ref[0] == 0, at[0], at[1])
    copy = pltpu.make_async_copy(volume_ref.at[pl.ds(first, count)], buffer, arrived)
    copy.start()
    copy.wait()
    pattern = tile_rows(spread_ref[...], buffer.shape[1])
    for p in range(count):
        wire_ref[p] = (buffer[p] * pattern).astype(BF16)


def blur_rows(planes, mx, my):
    return mul3(split(mul3(mx, split(planes))), my)


def z_rows(own, sib_refs, at, half, wo, ws, unspread):
    total = mul3(wo, split(own))
    sib = [r[:, pl.ds(at, 16), :].astype(F32)[:, half * GROUP:(half + 1) * GROUP] for r in sib_refs]
    sib = [a.reshape(a.shape[0] * GROUP, -1) for a in sib]
    rest = ws[0].shape[1] - sum(a.shape[0] for a in sib)
    sib = jnp.concatenate(sib + [jnp.zeros((rest, own.shape[1]), F32)], axis=0).astype(BF16)
    other = mul(ws[0], sib) + mul(ws[1], sib)
    scale = unspread[half * GROUP:(half + 1) * GROUP]
    return total + other * tile_rows(scale, other.shape[0])


def fill_z(own_refs, sib_refs, wo, ws, unspread_ref, far_ref, near_ref):
    unspread = unspread_ref[...]
    nx, ny = far_ref.shape[1:]

    def step(g, _):
        at = pl.multiple_of(g * 16, 16)
        for half in range(2):
            here = pl.ds(pl.multiple_of(at + half * GROUP, GROUP), GROUP)
            own = jnp.concatenate([r[:, here, :].reshape(r.shape[0] * GROUP, ny) for r in own_refs], axis=0)
            out = z_rows(own, sib_refs, at, half, wo, ws, unspread)
            cut = far_ref.shape[0] * GROUP
            far_ref[:, here, :] = out[:cut].reshape(far_ref.shape[0], GROUP, ny)
            near_ref[:, here, :] = out[cut:].reshape(near_ref.shape[0], GROUP, ny)
        return 0

    lax.fori_loop(0, nx // 16, step, 0, unroll=True)


def add_ext(ext_ref, we, unspread_ref, near_ref, out_ref):
    unspread = unspread_ref[...]
    n, nx, ny = near_ref.shape

    def step(g, _):
        at = pl.multiple_of(g * 16, 16)
        block = ext_ref[:, pl.ds(at, 16), :].astype(F32)
        for half in range(2):
            here = pl.ds(pl.multiple_of(at + half * GROUP, GROUP), GROUP)
            ext = block[:, half * GROUP:(half + 1) * GROUP].reshape(n * GROUP, ny)
            ext = jnp.concatenate([ext, jnp.zeros((we[0].shape[1] - n * GROUP, ny), F32)], axis=0).astype(BF16)
            other = (mul(we[0], ext) + mul(we[1], ext))[:n * GROUP]
            other = other * tile_rows(unspread[half * GROUP:(half + 1) * GROUP], n * GROUP)
            out_ref[:, here, :] = near_ref[:, here, :] + other.reshape(n, GROUP, ny)
        return 0

    lax.fori_loop(0, nx // 16, step, 0, unroll=True)


def to_quotient(load, count, core_ref, first, recorded_ref, m_ref, spread_ref, quotient_ref, wire_refs):
    mx, my = matrix(m_ref, X_FORWARD), matrix(m_ref, Y_FORWARD)
    pattern = tile_rows(spread_ref[...], recorded_ref.shape[1])
    first = jnp.where(core_ref[0] == 0, first[0], first[1])
    for p in range(count):
        quotient = recorded_ref[first + p].astype(F32) / blur_rows(load(p), mx, my)
        quotient_ref[p] = quotient
        wire, at = (wire_refs[0], p) if p < wire_refs[0].shape[0] else (wire_refs[1], p - wire_refs[0].shape[0])
        wire[at] = (quotient * pattern).astype(BF16)


def to_log(load, count, m_ref, log_ref):
    mx, my = matrix(m_ref, X_ADJOINT), matrix(m_ref, Y_ADJOINT)
    views, _, rows, ny = log_ref.shape
    for p in range(count):
        log_ref[:, p] = jnp.log(blur_rows(load(p), mx, my)).reshape(views, rows, ny)


def first_far_kernel(first, core_ref, start_ref, sib_a_ref, sib_b_ref, m_ref, unspread_ref, recorded_ref, spread_ref,
                     quotient_ref, wire_a_ref, wire_b_ref, near_ref, far_ref):
    own, sib = matrix(m_ref, OWN_FORWARD), matrix(m_ref, SIB_FORWARD)
    fill_z([start_ref], [sib_a_ref, sib_b_ref], own, sib, unspread_ref, far_ref, near_ref)
    to_quotient(lambda p: far_ref[p], quotient_ref.shape[0], core_ref, first, recorded_ref, m_ref, spread_ref,
                quotient_ref, [wire_a_ref, wire_b_ref])


def first_near_kernel(first, core_ref, near_ref, ext_ref, m_ref, unspread_ref, recorded_ref, spread_ref,
                      quotient_ref, wire_ref, sum_ref):
    add_ext(ext_ref, matrix(m_ref, EXT_FORWARD), unspread_ref, near_ref, sum_ref)
    to_quotient(lambda p: sum_ref[p], quotient_ref.shape[0], core_ref, first, recorded_ref, m_ref, spread_ref,
                quotient_ref, [wire_ref])


def block_kernel(block, first, core_ref, _, blocks_ref, m_ref, unspread_ref, recorded_ref, spread_ref, quotient_ref,
                 *wire_refs):
    views, _, rows, ny = blocks_ref.shape
    pattern = tile_rows(unspread_ref[...], views * rows)

    def load(p):
        return blocks_ref[:, block + p].reshape(views * rows, ny).astype(F32) * pattern

    to_quotient(load, quotient_ref.shape[0], core_ref, first, recorded_ref, m_ref, spread_ref, quotient_ref, wire_refs)


def adjoint_far_kernel(far_q_ref, near_q_ref, sib_a_ref, sib_b_ref, m_ref, unspread_ref, note_ref, log_ref, near_ref, far_ref):
    own, sib = matrix(m_ref, OWN_ADJOINT), matrix(m_ref, SIB_ADJOINT)
    fill_z([far_q_ref, near_q_ref], [sib_a_ref, sib_b_ref], own, sib, unspread_ref, far_ref, near_ref)
    to_log(lambda p: far_ref[p], far_ref.shape[0], m_ref, log_ref)
    for j in range(log_ref.shape[0] if log_ref.shape[1] > far_ref.shape[0] else 0):
        log_ref[j, far_ref.shape[0]] = note_ref[...]


def adjoint_near_kernel(near_ref, ext_ref, m_ref, unspread_ref, log_ref, sum_ref):
    add_ext(ext_ref, matrix(m_ref, EXT_ADJOINT), unspread_ref, near_ref, sum_ref)
    to_log(lambda p: sum_ref[p], sum_ref.shape[0], m_ref, log_ref)


def assemble_kernel(blocks_ref, out_ref):
    depth, rows, ny = out_ref.shape
    for z in range(depth):
        exponent = blocks_ref[0, depth + z // rows, z % rows:z % rows + 1, :]
        out_ref[z] = blocks_ref[0, z] * jnp.exp2(exponent - 15.0)


def assemble(blocks, depth):
    views, planes, rows, ny = blocks.shape
    return pl.pallas_call(
        assemble_kernel,
        grid=(views,),
        out_shape=jax.ShapeDtypeStruct((depth, views * rows, ny), F32),
        in_specs=[pl.BlockSpec((1, planes, rows, ny), lambda j: (j, 0, 0, 0))],
        out_specs=pl.BlockSpec((depth, rows, ny), lambda j: (0, j, 0)),
        compiler_params=pltpu.CompilerParams(vmem_limit_bytes=20 * 1024 * 1024),
        cost_estimate=LIGHT,
    )(blocks)


def to_other_chip(planes):
    count = lax.axis_size("gz")
    pairs = [(i, i + 1) for i in range(1, count - 1, 2)]
    return lax.ppermute(planes, "gz", pairs + [(b, a) for a, b in pairs])


def to_sibling(planes):
    count = lax.axis_size("gz")
    return lax.ppermute(planes, "gz", [(i, i ^ 1) for i in range(count)])


def to_views(blocks):
    return lax.all_to_all(blocks, "view", 0, 0)


def band(kernel_row, out_pos, in_pos):
    tap_index = in_pos[None, :] - out_pos[:, None] + RADIUS
    one_hot = (tap_index[:, :, None] == jnp.arange(TAPS, dtype=jnp.int32)[None, None, :]).astype(F32)
    return jnp.sum(one_hot * kernel_row[None, None, :], axis=2)


def gather_result(piece):
    views = lax.axis_size("view")
    depth, rows, ny = piece.shape
    extra = -(-depth // rows)
    exponent = jnp.maximum(jnp.ceil(jnp.log2(jnp.max(piece, axis=(1, 2)))), -100.0)
    scaled = piece * jnp.exp2(15.0 - exponent)[:, None, None]
    note = jnp.pad(exponent, (0, extra * rows - depth)).reshape(extra, rows, 1)
    note = jnp.broadcast_to(note, (extra, rows, ny))
    wire = jnp.concatenate([scaled, note], axis=0).astype(jnp.float16)
    return assemble(to_views(jnp.broadcast_to(wire[None], (views,) + wire.shape)).astype(F32), depth)


def per_device(views_data, psf, start):
    kernels = psf[0] / jnp.sum(psf[0], axis=1, keepdims=True)
    recorded = views_data[0]
    depth, nx, ny = recorded.shape
    views = lax.axis_size("view")
    v = lax.axis_index("view")
    core = lax.axis_index("gz") % 2
    rows = nx // views
    n_near, n_far = RADIUS, depth - RADIUS
    spread, unspread = jnp.asarray(SPREAD), jnp.asarray(UNSPREAD)

    near_at, far_at = (depth - n_near) * core, (depth - n_far) * (1 - core)

    def near_of(a):
        return lax.dynamic_slice_in_dim(a, near_at, n_near, axis=0)

    def far_of(a):
        return lax.dynamic_slice_in_dim(a, far_at, n_far, axis=0)

    def to_wire(planes):
        count = planes.shape[-2] // spread.shape[0]
        return (planes * jnp.concatenate([spread] * count, axis=0)).astype(BF16)

    core_at = core.reshape(1).astype(jnp.int32)
    far_planes, near_planes = (depth - n_far, 0), (0, depth - n_near)
    n_sib = n_far - n_far // 2
    far_shape, near_shape = (n_far, nx, ny), (n_near, nx, ny)
    sib_shapes = [((n_sib, nx, ny), BF16), ((n_far - n_sib, nx, ny), BF16)]

    (wire_near,) = call(
        lambda *refs: wire_kernel(near_planes, n_near, *refs),
        [(near_shape, BF16)],
        [core_at, start, spread],
        [pltpu.VMEM(near_shape, F32), pltpu.SemaphoreType.DMA],
        smem=1, far_off=(1,),
    )
    ext = to_other_chip(wire_near)
    (matrices,) = call(
        lambda *refs: band_kernel(n_near, n_far, *refs),
        [((MATRIX_ROWS, ny), F32)],
        [core_at, kernels, wire_near],
        smem=2, unread=(2,),
    )
    sib = []
    for i, (shape, dtype) in enumerate(sib_shapes):
        planes = tuple(at + i * n_sib for at in far_planes)
        (wire,) = call(
            lambda *refs: wire_kernel(planes, shape[0], *refs),
            [(shape, dtype)],
            [core_at, start, spread, wire_near],
            [pltpu.VMEM(shape, F32), pltpu.SemaphoreType.DMA],
            smem=1, far_off=(1,), unread=(3,),
        )
        sib.append(to_sibling(wire))

    quotient_far, wire_a, wire_b, partly = call(
        lambda *refs: first_far_kernel(far_planes, *refs),
        [(far_shape, F32)] + sib_shapes + [(near_shape, F32)],
        [core_at, start, *sib, matrices, unspread, recorded, spread],
        [pltpu.VMEM(far_shape, F32)],
        smem=1,
    )
    sib = [to_sibling(wire_a), to_sibling(wire_b)]
    quotient_near, wire_near = call(
        lambda *refs: first_near_kernel(near_planes, *refs),
        [(near_shape, F32), (near_shape, BF16)],
        [core_at, partly, ext, matrices, unspread, recorded, spread],
        [pltpu.VMEM(near_shape, F32)],
        smem=1, cost=HEAVY,
    )
    ext = to_other_chip(wire_near)

    count = jnp.arange(depth, dtype=jnp.int32)
    out_z = jnp.where(count < n_far, far_at + count, near_at + count - n_far)
    sib_z = count[:n_far] + jnp.where(core == 0, depth, -n_far)
    ext_z = count[:n_near] + jnp.where(core == 0, -n_near, depth)

    high = kernels[2].astype(jnp.float16).astype(F32)
    low = ((kernels[2] - high) * 2048.0).astype(jnp.float16).astype(F32)
    note = jnp.pad(jnp.stack([high, low]), ((0, rows - 2), (0, ny - TAPS)))

    for iteration in range(ITERS):
        extra = 1 if iteration == 0 else 0
        log_far, partly = call(
            adjoint_far_kernel,
            [((views, n_far + extra, rows, ny), F32), (near_shape, F32)],
            [quotient_far, quotient_near, *sib, matrices, unspread, note],
            [pltpu.VMEM(far_shape, F32)],
        )
        got = to_views(log_far.astype(jnp.float16))
        if iteration == 0:
            every_z = got[:, n_far, 0, :TAPS].astype(F32) + got[:, n_far, 1, :TAPS].astype(F32) / 2048.0
        sum_far = jnp.sum(got[:, :n_far].astype(F32), axis=0)

        (log_near,) = call(
            adjoint_near_kernel,
            [((views, n_near, rows, ny), F32)],
            [partly, ext, matrices, unspread],
            [pltpu.VMEM(near_shape, F32)],
            cost=HEAVY,
        )
        log_near, sum_far = lax.optimization_barrier((log_near.astype(jnp.float16), sum_far))
        if iteration == 0:
            own_rows = lax.dynamic_slice_in_dim(lax.optimization_barrier((start, log_near))[0], v * rows, rows, axis=1)
            piece_far, piece_near = far_of(own_rows), near_of(own_rows)
        piece_far = piece_far * jnp.exp(sum_far / views)
        piece_near = piece_near * jnp.exp(jnp.sum(to_views(log_near).astype(F32), axis=0) / views)

        if iteration < ITERS - 1:
            ext = to_other_chip(to_wire(piece_near))
            sib = to_sibling(to_wire(piece_far)).astype(F32) * unspread
            to_all = lambda planes, out, into: jnp.einsum(
                "zxy,voz->voxy", planes, jax.vmap(lambda row: band(row, out, into))(every_z), precision=lax.Precision.HIGH
            )
            blocks = to_all(jnp.concatenate([piece_far, piece_near, sib], axis=0), out_z, jnp.concatenate([out_z, sib_z]))
            extra = to_all(ext.astype(F32) * unspread, out_z[n_far:], ext_z)
            blocks = jnp.concatenate([to_wire(blocks[:, :n_far]), to_wire(blocks[:, n_far:] + extra)], axis=1)
            blocks = to_views(blocks)
            quotient_near, wire_near = call(
                lambda *refs: block_kernel(n_far, near_planes, *refs),
                [(near_shape, F32), (near_shape, BF16)],
                [core_at, core_at, blocks, matrices, unspread, recorded, spread],
                smem=2, cost=HEAVY,
            )
            ext = to_other_chip(wire_near)
            quotient_far, wire_a, wire_b = call(
                lambda *refs: block_kernel(0, far_planes, *refs),
                [(far_shape, F32)] + sib_shapes,
                [core_at, wire_near, blocks, matrices, unspread, recorded, spread],
                smem=1, unread=(1,),
            )
            sib = [to_sibling(wire_a), to_sibling(wire_b)]

    both = jnp.concatenate([piece_near, piece_far, piece_near], axis=0)
    return gather_result(lax.dynamic_slice_in_dim(both, n_near * core, depth, axis=0))


def solution(mesh):
    in_specs = (P("view", "gz", None, None), P("view", None, None), P("gz", None, None))
    out_specs = P("gz", None, None)
    return jax.shard_map(
        per_device, mesh=mesh, in_specs=in_specs, out_specs=out_specs, check_vma=False
    )
```

```python
import jax
import jax.numpy as jnp
import numpy as np
from jax import lax
from jax.experimental import pallas as pl
from jax.experimental.pallas import tpu as pltpu
from jax.sharding import PartitionSpec as P

RADIUS = 15
TAPS = 31
ITERS = 2
F32, BF16 = jnp.float32, jnp.bfloat16
GROUP = 8

_PHASE = np.arange(16)[:, None] * 0.7548776662 + np.arange(256)[None, :] * 0.5698402909
SPREAD = (1.0 + _PHASE % 1.0).astype(np.float32)
UNSPREAD = (1.0 / SPREAD.astype(np.float64)).astype(np.float32)


LIGHT = pl.CostEstimate(flops=1000, bytes_accessed=1000, transcendentals=0)
HEAVY = pl.CostEstimate(flops=6 * 10**10, bytes_accessed=2 * 10**8, transcendentals=0)


def call(kernel, outs, args, scratch=(), smem=0, anywhere=(), cost=LIGHT, limit=16):
    specs = [pl.BlockSpec(memory_space=pltpu.SMEM)] * smem
    specs += [pl.BlockSpec(memory_space=pl.ANY if i in anywhere else pltpu.VMEM) for i in range(smem, len(args))]
    return pl.pallas_call(
        kernel,
        out_shape=[jax.ShapeDtypeStruct(shape, dtype) for shape, dtype in outs],
        in_specs=specs,
        out_specs=[pl.BlockSpec(memory_space=pltpu.VMEM)] * len(outs),
        scratch_shapes=list(scratch),
        compiler_params=pltpu.CompilerParams(vmem_limit_bytes=limit * 1024 * 1024),
        cost_estimate=cost,
    )(*args)


def split(a):
    high = a.astype(BF16)
    return high, (a - high.astype(F32)).astype(BF16)


def mul(a, b):
    return jnp.dot(a, b, preferred_element_type=F32)


def mul3(a, b):
    return mul(a[0], b[0]) + mul(a[0], b[1]) + mul(a[1], b[0])


def tile_rows(pattern, rows):
    return jnp.concatenate([pattern] * (rows // pattern.shape[0]), axis=0)


X_FORWARD, X_ADJOINT = (0, 0, 128, 128), (0, 128, 128, 128)
Y_FORWARD, Y_ADJOINT = (128, 0, 256, 256), (384, 0, 256, 256)
OWN_FORWARD, OWN_ADJOINT = (640, 0, 256, 256), (896, 0, 256, 256)
SIB_FORWARD, SIB_ADJOINT = (1152, 0, 256, 144), (1408, 0, 256, 144)
EXT_FORWARD, EXT_ADJOINT = (1664, 0, 120, 128), (1664, 128, 120, 128)
MATRIX_ROWS = 1784


def matrix(ref, where):
    row, column, rows, columns = where
    return split(ref[row:row + rows, column:column + columns])


def band_kernel(n_near, n_far, core_ref, taps_ref, _, out_ref):
    depth = n_near + n_far
    core = core_ref[0]
    near_at, far_at = (depth - n_near) * core, (depth - n_far) * (1 - core)
    natural = lambda i: i
    ordered = lambda i: jnp.where(i < n_far, far_at + i, near_at + i - n_far)
    near = lambda i: near_at + i
    ext = lambda i: i + jnp.where(core == 0, -n_near, depth)
    sib = lambda i: jnp.where(i < n_far, i + jnp.where(core == 0, depth, -n_far), 4 * depth)
    plans = [
        (X_FORWARD, 0, natural, natural, 1, 1), (X_ADJOINT, 0, natural, natural, -1, 1),
        (Y_FORWARD, 1, natural, natural, -1, 1), (Y_ADJOINT, 1, natural, natural, 1, 1),
        (OWN_FORWARD, 2, ordered, natural, 1, GROUP), (OWN_ADJOINT, 2, ordered, ordered, -1, GROUP),
        (SIB_FORWARD, 2, ordered, sib, 1, GROUP), (SIB_ADJOINT, 2, ordered, sib, -1, GROUP),
        (EXT_FORWARD, 2, near, ext, 1, GROUP), (EXT_ADJOINT, 2, near, ext, -1, GROUP),
    ]
    for (at, column_at, rows, columns), axis, out_pos, in_pos, direction, repeat in plans:
        columns = -(-columns // 128) * 128
        row = lax.broadcasted_iota(jnp.int32, (rows, columns), 0)
        column = lax.broadcasted_iota(jnp.int32, (rows, columns), 1)
        tap = direction * (in_pos(column // repeat) - out_pos(row // repeat)) + RADIUS
        if repeat > 1:
            tap = jnp.where(row % repeat == column % repeat, tap, -1)
        total = jnp.zeros((rows, columns), F32)
        for k in range(TAPS):
            total = total + jnp.where(tap == k, taps_ref[axis, k], 0.0)
        out_ref[at:at + rows, column_at:column_at + columns] = total


def wire_kernel(at, count, core_ref, volume_ref, spread_ref, *refs):
    wire_ref, buffer, arrived = refs[-3:]
    first = jnp.where(core_ref[0] == 0, at[0], at[1])
    copy = pltpu.make_async_copy(volume_ref.at[pl.ds(first, count)], buffer, arrived)
    copy.start()
    copy.wait()
    pattern = tile_rows(spread_ref[...], buffer.shape[1])
    for p in range(count):
        wire_ref[p] = (buffer[p] * pattern).astype(BF16)


def blur_rows(planes, mx, my):
    return mul3(split(mul3(mx, split(planes))), my)


def z_rows(own, sib_refs, at, half, wo, ws, unspread):
    total = mul3(wo, split(own))
    sib = [r[:, pl.ds(at, 16), :].astype(F32)[:, half * GROUP:(half + 1) * GROUP] for r in sib_refs]
    sib = [a.reshape(a.shape[0] * GROUP, -1) for a in sib]
    rest = ws[0].shape[1] - sum(a.shape[0] for a in sib)
    sib = jnp.concatenate(sib + [jnp.zeros((rest, own.shape[1]), F32)], axis=0).astype(BF16)
    other = mul(ws[0], sib) + mul(ws[1], sib)
    scale = unspread[half * GROUP:(half + 1) * GROUP]
    return total + other * tile_rows(scale, other.shape[0])


def fill_z(own_refs, sib_refs, wo, ws, unspread_ref, far_ref, near_ref):
    unspread = unspread_ref[...]
    nx, ny = far_ref.shape[1:]

    def step(g, _):
        at = pl.multiple_of(g * 16, 16)
        for half in range(2):
            here = pl.ds(pl.multiple_of(at + half * GROUP, GROUP), GROUP)
            own = jnp.concatenate([r[:, here, :].reshape(r.shape[0] * GROUP, ny) for r in own_refs], axis=0)
            out = z_rows(own, sib_refs, at, half, wo, ws, unspread)
            cut = far_ref.shape[0] * GROUP
            far_ref[:, here, :] = out[:cut].reshape(far_ref.shape[0], GROUP, ny)
            near_ref[:, here, :] = out[cut:].reshape(near_ref.shape[0], GROUP, ny)
        return 0

    lax.fori_loop(0, nx // 16, step, 0, unroll=True)


def add_ext(ext_ref, we, unspread_ref, near_ref, out_ref):
    unspread = unspread_ref[...]
    n, nx, ny = near_ref.shape

    def step(g, _):
        at = pl.multiple_of(g * 16, 16)
        block = ext_ref[:, pl.ds(at, 16), :].astype(F32)
        for half in range(2):
            here = pl.ds(pl.multiple_of(at + half * GROUP, GROUP), GROUP)
            ext = block[:, half * GROUP:(half + 1) * GROUP].reshape(n * GROUP, ny)
            ext = jnp.concatenate([ext, jnp.zeros((we[0].shape[1] - n * GROUP, ny), F32)], axis=0).astype(BF16)
            other = (mul(we[0], ext) + mul(we[1], ext))[:n * GROUP]
            other = other * tile_rows(unspread[half * GROUP:(half + 1) * GROUP], n * GROUP)
            out_ref[:, here, :] = near_ref[:, here, :] + other.reshape(n, GROUP, ny)
        return 0

    lax.fori_loop(0, nx // 16, step, 0, unroll=True)


def to_quotient(load, count, core_ref, first, recorded_ref, m_ref, spread_ref, quotient_ref, wire_refs):
    mx, my = matrix(m_ref, X_FORWARD), matrix(m_ref, Y_FORWARD)
    pattern = tile_rows(spread_ref[...], recorded_ref.shape[1])
    first = jnp.where(core_ref[0] == 0, first[0], first[1])
    for p in range(count):
        quotient = recorded_ref[first + p].astype(F32) / blur_rows(load(p), mx, my)
        quotient_ref[p] = quotient
        wire, at = (wire_refs[0], p) if p < wire_refs[0].shape[0] else (wire_refs[1], p - wire_refs[0].shape[0])
        wire[at] = (quotient * pattern).astype(BF16)


def to_log(load, count, m_ref, log_ref):
    mx, my = matrix(m_ref, X_ADJOINT), matrix(m_ref, Y_ADJOINT)
    views, _, rows, ny = log_ref.shape
    for p in range(count):
        log_ref[:, p] = jnp.log(blur_rows(load(p), mx, my)).reshape(views, rows, ny)


def first_far_kernel(first, core_ref, start_ref, sib_a_ref, sib_b_ref, m_ref, unspread_ref, recorded_ref, spread_ref,
                     quotient_ref, wire_ref, near_ref, far_ref):
    own, sib = matrix(m_ref, OWN_FORWARD), matrix(m_ref, SIB_FORWARD)
    fill_z([start_ref], [sib_a_ref, sib_b_ref], own, sib, unspread_ref, far_ref, near_ref)
    to_quotient(lambda p: far_ref[p], quotient_ref.shape[0], core_ref, first, recorded_ref, m_ref, spread_ref,
                quotient_ref, [wire_ref])


def first_near_kernel(first, core_ref, near_ref, ext_ref, m_ref, unspread_ref, recorded_ref, spread_ref,
                      quotient_ref, wire_ref, sum_ref):
    add_ext(ext_ref, matrix(m_ref, EXT_FORWARD), unspread_ref, near_ref, sum_ref)
    to_quotient(lambda p: sum_ref[p], quotient_ref.shape[0], core_ref, first, recorded_ref, m_ref, spread_ref,
                quotient_ref, [wire_ref])


def block_kernel(block, first, core_ref, _, blocks_ref, m_ref, unspread_ref, recorded_ref, spread_ref, quotient_ref,
                 *wire_refs):
    views, _, rows, ny = blocks_ref.shape
    pattern = tile_rows(unspread_ref[...], views * rows)

    def load(p):
        return blocks_ref[:, block + p].reshape(views * rows, ny).astype(F32) * pattern

    to_quotient(load, quotient_ref.shape[0], core_ref, first, recorded_ref, m_ref, spread_ref, quotient_ref, wire_refs)


def adjoint_far_kernel(far_q_ref, near_q_ref, *refs):
    *sib_refs, m_ref, unspread_ref, note_ref, log_ref, near_ref, far_ref = refs
    own, sib = matrix(m_ref, OWN_ADJOINT), matrix(m_ref, SIB_ADJOINT)
    fill_z([far_q_ref, near_q_ref], sib_refs, own, sib, unspread_ref, far_ref, near_ref)
    to_log(lambda p: far_ref[p], far_ref.shape[0], m_ref, log_ref)
    for j in range(log_ref.shape[0] if log_ref.shape[1] > far_ref.shape[0] else 0):
        log_ref[j, far_ref.shape[0]] = note_ref[...]


def adjoint_near_kernel(near_ref, ext_ref, m_ref, unspread_ref, log_ref, sum_ref):
    add_ext(ext_ref, matrix(m_ref, EXT_ADJOINT), unspread_ref, near_ref, sum_ref)
    to_log(lambda p: sum_ref[p], sum_ref.shape[0], m_ref, log_ref)


def rows_kernel(at, view_ref, volume_ref, _, far_ref, near_ref, arrived):
    core, first = view_ref[0], pl.multiple_of(view_ref[1] * far_ref.shape[1], far_ref.shape[1])
    copies = []
    for i, ref in enumerate((far_ref, near_ref)):
        planes = jnp.where(core == 0, at[i][0], at[i][1])
        source = volume_ref.at[pl.ds(planes, ref.shape[0]), pl.ds(first, ref.shape[1]), :]
        copies.append(pltpu.make_async_copy(source, ref, arrived.at[i]))
    for copy in copies:
        copy.start()
    for copy in copies:
        copy.wait()


def assemble_kernel(blocks_ref, out_ref):
    depth, rows, ny = out_ref.shape
    for z in range(depth):
        exponent = blocks_ref[0, depth, z % rows:z % rows + 1, :]
        half = exponent[:, :ny // 2] if z < rows else exponent[:, ny // 2:]
        out_ref[z] = blocks_ref[0, z] * jnp.exp2(jnp.concatenate([half, half], axis=1) - 15.0)


def assemble(blocks, depth):
    views, planes, rows, ny = blocks.shape
    return pl.pallas_call(
        assemble_kernel,
        grid=(views,),
        out_shape=jax.ShapeDtypeStruct((depth, views * rows, ny), F32),
        in_specs=[pl.BlockSpec((1, planes, rows, ny), lambda j: (j, 0, 0, 0))],
        out_specs=pl.BlockSpec((depth, rows, ny), lambda j: (0, j, 0)),
        compiler_params=pltpu.CompilerParams(vmem_limit_bytes=20 * 1024 * 1024),
        cost_estimate=LIGHT,
    )(blocks)


def to_other_chip(planes):
    count = lax.axis_size("gz")
    pairs = [(i, i + 1) for i in range(1, count - 1, 2)]
    return lax.ppermute(planes, "gz", pairs + [(b, a) for a, b in pairs])


def to_sibling(planes):
    count = lax.axis_size("gz")
    return lax.ppermute(planes, "gz", [(i, i ^ 1) for i in range(count)])


def to_views(blocks):
    return lax.all_to_all(blocks, "view", 0, 0)


def sum_over_x(log_blocks):
    views = lax.axis_size("view")
    groups = [list(range(z, views, 2)) for z in range(2)]
    blocks = log_blocks.reshape((views // 2, 2) + log_blocks.shape[1:])
    return lax.all_to_all(blocks, "view", 0, 0, axis_index_groups=groups)


def to_z_partner(block):
    return lax.ppermute(block, "view", [(i, i ^ 1) for i in range(lax.axis_size("view"))])


def band(kernel_row, out_pos, in_pos):
    tap_index = in_pos[None, :] - out_pos[:, None] + RADIUS
    one_hot = (tap_index[:, :, None] == jnp.arange(TAPS, dtype=jnp.int32)[None, None, :]).astype(F32)
    return jnp.sum(one_hot * kernel_row[None, None, :], axis=2)


def gather_result(piece):
    views = lax.axis_size("view")
    depth, rows, ny = piece.shape
    exponent = jnp.maximum(jnp.ceil(jnp.log2(jnp.max(piece, axis=(1, 2)))), -100.0)
    scaled = piece * jnp.exp2(15.0 - exponent)[:, None, None]
    note = jnp.broadcast_to(exponent.reshape(depth // rows, rows, 1), (depth // rows, rows, ny * rows // depth))
    note = jnp.concatenate(list(note), axis=1)[None]
    wire = jnp.concatenate([scaled, note], axis=0).astype(jnp.float16)
    return assemble(to_views(jnp.broadcast_to(wire[None], (views,) + wire.shape)).astype(F32), depth)


def per_device(views_data, psf, start):
    kernels = psf[0] / jnp.sum(psf[0], axis=1, keepdims=True)
    recorded = views_data[0]
    depth, nx, ny = recorded.shape
    views = lax.axis_size("view")
    v = lax.axis_index("view")
    core = lax.axis_index("gz") % 2
    z_lo = v % 2
    rows = nx // views
    n_near, n_far = RADIUS, depth - RADIUS
    spread, unspread = jnp.asarray(SPREAD), jnp.asarray(UNSPREAD)

    near_at, far_at = (depth - n_near) * core, (depth - n_far) * (1 - core)

    def to_wire(planes):
        count = planes.shape[-2] // spread.shape[0]
        return (planes * jnp.concatenate([spread] * count, axis=0)).astype(BF16)

    core_at = core.reshape(1).astype(jnp.int32)
    far_planes, near_planes = (depth - n_far, 0), (0, depth - n_near)
    n_sib = n_far - n_far // 2
    far_shape, near_shape = (n_far, nx, ny), (n_near, nx, ny)
    sib_shapes = [((n_sib, nx, ny), BF16), ((n_far - n_sib, nx, ny), BF16)]

    (wire_near,) = call(
        lambda *refs: wire_kernel(near_planes, n_near, *refs),
        [(near_shape, BF16)],
        [core_at, start, spread],
        [pltpu.VMEM(near_shape, F32), pltpu.SemaphoreType.DMA],
        smem=1, anywhere=(1,),
    )
    ext = to_other_chip(wire_near)
    (matrices,) = call(
        lambda *refs: band_kernel(n_near, n_far, *refs),
        [((MATRIX_ROWS, ny), F32)],
        [core_at, kernels, wire_near],
        smem=2, anywhere=(2,),
    )
    sib = []
    for i, (shape, dtype) in enumerate(sib_shapes):
        planes = tuple(at + i * n_sib for at in far_planes)
        (wire,) = call(
            lambda *refs: wire_kernel(planes, shape[0], *refs),
            [(shape, dtype)],
            [core_at, start, spread, wire_near],
            [pltpu.VMEM(shape, F32), pltpu.SemaphoreType.DMA],
            smem=1, anywhere=(1, 3),
        )
        sib.append(to_sibling(wire))

    quotient_far, wire_far, partly = call(
        lambda *refs: first_far_kernel(far_planes, *refs),
        [(far_shape, F32), (far_shape, BF16), (near_shape, F32)],
        [core_at, start, *sib, matrices, unspread, recorded, spread],
        [pltpu.VMEM(far_shape, F32)],
        smem=1,
    )
    sib = [to_sibling(wire_far)]
    quotient_near, wire_near = call(
        lambda *refs: first_near_kernel(near_planes, *refs),
        [(near_shape, F32), (near_shape, BF16)],
        [core_at, partly, ext, matrices, unspread, recorded, spread],
        [pltpu.VMEM(near_shape, F32)],
        smem=1, cost=HEAVY,
    )
    ext = to_other_chip(wire_near)

    count = jnp.arange(depth, dtype=jnp.int32)
    out_z = jnp.where(count < n_far, far_at + count, near_at + count - n_far)
    sib_z = count[:n_far] + jnp.where(core == 0, depth, -n_far)
    ext_z = count[:n_near] + jnp.where(core == 0, -n_near, depth)

    high = kernels[2].astype(jnp.float16).astype(F32)
    low = ((kernels[2] - high) * 2048.0).astype(jnp.float16).astype(F32)
    note = jnp.pad(jnp.stack([high, low]), ((0, rows - 2), (0, ny - TAPS)))

    for iteration in range(ITERS):
        extra = 1 if iteration == 0 else 0
        log_far, partly = call(
            adjoint_far_kernel,
            [((views, n_far + extra, rows, ny), F32), (near_shape, F32)],
            [quotient_far, quotient_near, *sib, matrices, unspread, note],
            [pltpu.VMEM(far_shape, F32)],
        )
        got = sum_over_x(log_far.astype(jnp.float16))
        sums = jnp.sum(got[:, :, :n_far].astype(F32), axis=0)
        own_sum, other = jnp.where(z_lo == 0, sums[0], sums[1]), jnp.where(z_lo == 0, sums[1], sums[0])
        other = other.astype(jnp.float16)

        (log_near,) = call(
            adjoint_near_kernel,
            [((views, n_near, rows, ny), F32)],
            [partly, ext, matrices, unspread],
            [pltpu.VMEM(near_shape, F32)],
            cost=HEAVY,
        )
        log_near, other, own_sum = lax.optimization_barrier((log_near.astype(jnp.float16), other, own_sum))
        if iteration == 0:
            mine = got[:, 0, n_far, :2, :TAPS].reshape(views, TAPS)
            mine_planes = jnp.pad(mine, ((0, rows - views), (0, ny - TAPS)))[None]
            other = to_z_partner(jnp.concatenate([other, mine_planes], axis=0))
            pair = [mine.astype(F32), other[n_far, :views, :TAPS].astype(F32)]
            pair = [t.reshape(views // 2, 2, TAPS) for t in pair]
            pair = [t[:, 0] + t[:, 1] / 2048.0 for t in pair]
            every_z = jnp.where(z_lo == 0, jnp.stack(pair, axis=1), jnp.stack(pair[::-1], axis=1)).reshape(views, TAPS)
            other = other[:n_far]
            piece_far, piece_near = call(
                lambda *refs: rows_kernel((far_planes, near_planes), *refs),
                [((n_far, rows, ny), F32), ((n_near, rows, ny), F32)],
                [jnp.stack([core, v]).astype(jnp.int32), start, own_sum],
                [pltpu.SemaphoreType.DMA((2,))],
                smem=1, anywhere=(1, 2), limit=56,
            )
        else:
            other = to_z_partner(other)
        piece_far = piece_far * jnp.exp((own_sum + other.astype(F32)) / views)
        piece_near = piece_near * jnp.exp(jnp.sum(to_views(log_near).astype(F32), axis=0) / views)

        if iteration < ITERS - 1:
            ext = to_other_chip(to_wire(piece_near))
            sib = to_sibling(to_wire(piece_far)).astype(F32) * unspread
            to_all = lambda planes, out, into: jnp.einsum(
                "zxy,voz->voxy", planes, jax.vmap(lambda row: band(row, out, into))(every_z), precision=lax.Precision.HIGH
            )
            blocks = to_all(jnp.concatenate([piece_far, piece_near, sib], axis=0), out_z, jnp.concatenate([out_z, sib_z]))
            extra = to_all(ext.astype(F32) * unspread, out_z[n_far:], ext_z)
            blocks = jnp.concatenate([to_wire(blocks[:, :n_far]), to_wire(blocks[:, n_far:] + extra)], axis=1)
            blocks = to_views(blocks)
            quotient_near, wire_near = call(
                lambda *refs: block_kernel(n_far, near_planes, *refs),
                [(near_shape, F32), (near_shape, BF16)],
                [core_at, core_at, blocks, matrices, unspread, recorded, spread],
                smem=2, cost=HEAVY,
            )
            ext = to_other_chip(wire_near)
            quotient_far, wire_a, wire_b = call(
                lambda *refs: block_kernel(0, far_planes, *refs),
                [(far_shape, F32)] + sib_shapes,
                [core_at, wire_near, blocks, matrices, unspread, recorded, spread],
                smem=1, anywhere=(1,),
            )
            sib = [to_sibling(wire_a), to_sibling(wire_b)]

    both = jnp.concatenate([piece_near, piece_far, piece_near], axis=0)
    return gather_result(lax.dynamic_slice_in_dim(both, n_near * core, depth, axis=0))


def solution(mesh):
    in_specs = (P("view", "gz", None, None), P("view", None, None), P("gz", None, None))
    out_specs = P("gz", None, None)
    return jax.shard_map(
        per_device, mesh=mesh, in_specs=in_specs, out_specs=out_specs, check_vma=False
    )
```

```python
import jax
import jax.numpy as jnp
import numpy as np
from jax import lax
from jax.experimental import pallas as pl
from jax.experimental.pallas import tpu as pltpu
from jax.sharding import PartitionSpec as P

RADIUS = 15
TAPS = 31
ITERS = 2
F32, BF16 = jnp.float32, jnp.bfloat16
GROUP = 8

ROW_STEP, COLUMN_STEP = 49471, 37345
_PHASE = np.arange(16)[:, None] * ROW_STEP + np.arange(256)[None, :] * COLUMN_STEP
SPREAD = (1.0 + (_PHASE % 65536) / 65536.0).astype(np.float32)
UNSPREAD = (1.0 / SPREAD.astype(np.float64)).astype(np.float32)


def spread_pattern(shape):
    row, column = lax.broadcasted_iota(jnp.int32, shape, 0), lax.broadcasted_iota(jnp.int32, shape, 1)
    return 1.0 + ((row * ROW_STEP + column * COLUMN_STEP) % 65536).astype(F32) / 65536.0


LIGHT = pl.CostEstimate(flops=1000, bytes_accessed=1000, transcendentals=0)
HEAVY = pl.CostEstimate(flops=6 * 10**10, bytes_accessed=2 * 10**8, transcendentals=0)


def call(kernel, outs, args, scratch=(), smem=0, anywhere=(), hbm=(), hbm_out=(), cost=LIGHT, limit=20):
    anywhere = set(anywhere) | set(hbm)
    specs = [pl.BlockSpec(memory_space=pltpu.SMEM)] * smem
    specs += [pl.BlockSpec(memory_space=pl.ANY if i in anywhere else pltpu.VMEM) for i in range(smem, len(args))]
    args = [pltpu.with_memory_space_constraint(a, pltpu.HBM) if i in hbm else a for i, a in enumerate(args)]
    return pl.pallas_call(
        kernel,
        out_shape=[
            (pltpu.HBM if i in hbm_out else jax.ShapeDtypeStruct)(shape, dtype) for i, (shape, dtype) in enumerate(outs)
        ],
        in_specs=specs,
        out_specs=[
            pl.BlockSpec(memory_space=pl.ANY if i in hbm_out else pltpu.VMEM) for i in range(len(outs))
        ],
        scratch_shapes=list(scratch),
        compiler_params=pltpu.CompilerParams(vmem_limit_bytes=limit * 1024 * 1024),
        cost_estimate=cost,
    )(*args)


def split(a):
    high = a.astype(BF16)
    return high, (a - high.astype(F32)).astype(BF16)


def mul(a, b):
    return jnp.dot(a, b, preferred_element_type=F32)


def mul3(a, b):
    return mul(a[0], b[0]) + mul(a[0], b[1]) + mul(a[1], b[0])


def tile_rows(pattern, rows):
    return jnp.concatenate([pattern] * (rows // pattern.shape[0]), axis=0)


X_FORWARD, X_ADJOINT = (0, 0, 128, 128), (0, 128, 128, 128)
Y_FORWARD, Y_ADJOINT = (128, 0, 256, 256), (384, 0, 256, 256)
OWN_FORWARD, OWN_ADJOINT = (640, 0, 256, 256), (896, 0, 256, 256)
SIB_FORWARD, SIB_ADJOINT = (1152, 0, 136, 144), (1288, 0, 136, 144)
EXT_FORWARD, EXT_ADJOINT = (1424, 0, 120, 128), (1424, 128, 120, 128)
MATRIX_ROWS = 1544


def matrix(ref, where):
    row, column, rows, columns = where
    return split(ref[row:row + rows, column:column + columns])


def band_kernel(n_near, n_far, core_ref, taps_ref, _, out_ref):
    depth = n_near + n_far
    core = core_ref[0]
    near_at, far_at = (depth - n_near) * core, (depth - n_far) * (1 - core)
    natural = lambda i: i
    ordered = lambda i: jnp.where(i < n_far, far_at + i, near_at + i - n_far)
    near = lambda i: near_at + i
    ext = lambda i: i + jnp.where(core == 0, -n_near, depth)
    sib = lambda i: jnp.where(i < n_far, i + jnp.where(core == 0, depth, -n_far), 4 * depth)
    plans = [
        (X_FORWARD, 0, natural, natural, 1, 1), (X_ADJOINT, 0, natural, natural, -1, 1),
        (Y_FORWARD, 1, natural, natural, -1, 1), (Y_ADJOINT, 1, natural, natural, 1, 1),
        (OWN_FORWARD, 2, ordered, natural, 1, GROUP), (OWN_ADJOINT, 2, ordered, ordered, -1, GROUP),
        (SIB_FORWARD, 2, ordered, sib, 1, GROUP), (SIB_ADJOINT, 2, ordered, sib, -1, GROUP),
        (EXT_FORWARD, 2, near, ext, 1, GROUP), (EXT_ADJOINT, 2, near, ext, -1, GROUP),
    ]
    for (at, column_at, rows, columns), axis, out_pos, in_pos, direction, repeat in plans:
        columns = -(-columns // 128) * 128
        row = lax.broadcasted_iota(jnp.int32, (rows, columns), 0)
        column = lax.broadcasted_iota(jnp.int32, (rows, columns), 1)
        tap = direction * (in_pos(column // repeat) - out_pos(row // repeat)) + RADIUS
        if repeat > 1:
            tap = jnp.where(row % repeat == column % repeat, tap, -1)
        total = jnp.zeros((rows, columns), F32)
        for k in range(TAPS):
            total = total + jnp.where(tap == k, taps_ref[axis, k], 0.0)
        out_ref[at:at + rows, column_at:column_at + columns] = total


def wire_kernel(at, core_ref, volume_ref, *refs):
    *wire_refs, buffer, arrived = refs
    first = jnp.where(core_ref[0] == 0, at[0], at[1])
    count, step = buffer.shape[0], -(-buffer.shape[0] // arrived.shape[0])
    parts = [slice(p, min(p + step, count)) for p in range(0, count, step)]
    copies = [
        pltpu.make_async_copy(volume_ref.at[pl.ds(first + r.start, r.stop - r.start)], buffer.at[r], arrived.at[i])
        for i, r in enumerate(parts)
    ]
    for copy in copies:
        copy.start()
    pattern = tile_rows(spread_pattern((16, buffer.shape[2])), buffer.shape[1])
    done = 0
    for wire_ref in wire_refs:
        for p in range(wire_ref.shape[0]):
            if done % step == 0:
                copies[done // step].wait()
            wire_ref[p] = (buffer[done] * pattern).astype(BF16)
            done += 1


def blur_rows(planes, mx, my):
    return mul3(split(mul3(mx, split(planes))), my)


def own_rows_z(own, wo):
    return mul3(wo, split(own))


def sib_rows_z(sib_refs, at, half, ws, unspread):
    sib = [r[:, pl.ds(at, 16), :].astype(F32)[:, half * GROUP:(half + 1) * GROUP] for r in sib_refs]
    sib = [a.reshape(a.shape[0] * GROUP, -1) for a in sib]
    rest = ws[0].shape[1] - sum(a.shape[0] for a in sib)
    sib = jnp.concatenate(sib + [jnp.zeros((rest, sib[0].shape[1]), F32)], axis=0).astype(BF16)
    other = mul(ws[0], sib) + mul(ws[1], sib)
    return other * tile_rows(unspread[half * GROUP:(half + 1) * GROUP], other.shape[0])


def fill_z(own_refs, sib_refs, wo, ws, unspread_ref, far_ref, near_ref, before=None, after=None):
    nx, ny = far_ref.shape[1:]
    cut = far_ref.shape[0] * GROUP
    for at in range(0, nx, 16):
        if before:
            before(at)
        for half in range(2):
            here = slice(at + half * GROUP, at + (half + 1) * GROUP)
            own = jnp.concatenate([r[:, here, :].reshape(r.shape[0] * GROUP, ny) for r in own_refs], axis=0)
            out = own_rows_z(own, wo)
            far = out[:cut]
            if sib_refs:
                far = far + sib_rows_z(sib_refs, at, half, ws, unspread_ref[...])
            far_ref[:, here, :] = far.reshape(far_ref.shape[0], GROUP, ny)
            near_ref[:, here, :] = out[cut:].reshape(near_ref.shape[0], GROUP, ny)
        if after:
            after(at)


def add_sib(sib_refs, ws, unspread_ref, far_in_ref, far_ref):
    n, nx, ny = far_ref.shape

    def step(g, _):
        at = pl.multiple_of(g * 16, 16)
        for half in range(2):
            here = pl.ds(pl.multiple_of(at + half * GROUP, GROUP), GROUP)
            other = sib_rows_z(sib_refs, at, half, ws, unspread_ref[...])
            far_ref[:, here, :] = far_in_ref[:, here, :] + other.reshape(n, GROUP, ny)
        return 0

    lax.fori_loop(0, nx // 16, step, 0, unroll=True)


def copies_by_rows(source, target, done):
    rows = [slice(at, at + 16) for at in range(0, source.shape[1], 16)]
    return {r.start: pltpu.make_async_copy(source.at[:, r, :], target.at[:, r, :], done.at[i]) for i, r in enumerate(rows)}


def planes_from(first, core_ref, ref):
    at = jnp.where(core_ref[0] == 0, first[0], first[1])
    return lambda p: ref[at + p]


def ext_z(ext_ref, we, unspread_ref, out_ref):
    n, nx, ny = out_ref.shape
    for at in range(0, nx, 2 * GROUP):
        block = ext_ref[:, at:at + 2 * GROUP, :].astype(F32)
        for half in range(2):
            ext = block[:, half * GROUP:(half + 1) * GROUP].reshape(n * GROUP, ny)
            ext = jnp.concatenate([ext, jnp.zeros((we[0].shape[1] - n * GROUP, ny), F32)], axis=0).astype(BF16)
            other = mul(we[0], ext) + mul(we[1], ext)
            other = other * tile_rows(unspread_ref[half * GROUP:(half + 1) * GROUP], n * GROUP)
            here = slice(at + half * GROUP, at + (half + 1) * GROUP)
            out_ref[:, here, :] = other.reshape(n, GROUP, ny)


def to_quotient(load, recorded, m_ref, spread_ref, quotient_ref, wire_refs):
    mx, my = matrix(m_ref, X_FORWARD), matrix(m_ref, Y_FORWARD)
    pattern = tile_rows(spread_ref[...], quotient_ref.shape[1])
    for p in range(quotient_ref.shape[0]):
        quotient = recorded(p).astype(F32) / blur_rows(load(p), mx, my)
        quotient_ref[p] = quotient
        wire, at = (wire_refs[0], p) if p < wire_refs[0].shape[0] else (wire_refs[1], p - wire_refs[0].shape[0])
        wire[at] = (quotient * pattern).astype(BF16)


def to_log(load, count, m_ref, log_ref):
    mx, my = matrix(m_ref, X_ADJOINT), matrix(m_ref, Y_ADJOINT)
    views, _, rows, ny = log_ref.shape
    for p in range(count):
        log_ref[:, p] = jnp.log(blur_rows(load(p), mx, my)).reshape(views, rows, ny)


def first_far_kernel(first, core_ref, start_ref, sib_a_ref, sib_b_ref, m_ref, unspread_ref, recorded_ref, spread_ref,
                     quotient_ref, wire_ref, near_ref, far_ref, recorded, recorded_done, start, start_done):
    copies = copies_by_rows(start_ref, start, start_done)
    for copy in copies.values():
        copy.start()
    planes = pl.ds(jnp.where(core_ref[0] == 0, first[0], first[1]), recorded.shape[0])
    copy = pltpu.make_async_copy(recorded_ref.at[planes], recorded, recorded_done)
    copy.start()
    own, sib = matrix(m_ref, OWN_FORWARD), matrix(m_ref, SIB_FORWARD)
    fill_z([start], [sib_a_ref, sib_b_ref], own, sib, unspread_ref, far_ref, near_ref, before=lambda at: copies[at].wait())
    copy.wait()
    to_quotient(lambda p: far_ref[p], lambda p: recorded[p], m_ref, spread_ref, quotient_ref, [wire_ref])


def first_near_kernel(first, core_ref, near_ref, ext_ref, m_ref, unspread_ref, recorded_ref, spread_ref,
                      quotient_ref, wire_ref, sum_ref):
    ext_z(ext_ref, matrix(m_ref, EXT_FORWARD), unspread_ref, sum_ref)
    recorded = planes_from(first, core_ref, recorded_ref)
    to_quotient(lambda p: near_ref[p] + sum_ref[p], recorded, m_ref, spread_ref, quotient_ref, [wire_ref])


def block_kernel(block, first, core_ref, _, blocks_ref, m_ref, unspread_ref, recorded_ref, spread_ref, quotient_ref, *wire_refs):
    views, _, rows, ny = blocks_ref.shape
    pattern = tile_rows(unspread_ref[...], views * rows)

    def load(p):
        return blocks_ref[:, block + p].reshape(views * rows, ny).astype(F32) * pattern

    to_quotient(load, planes_from(first, core_ref, recorded_ref), m_ref, spread_ref, quotient_ref, wire_refs)


def adjoint_own_kernel(far_q_ref, near_q_ref, m_ref, far_ref, near_out_ref, near_ref, sent):
    copies = copies_by_rows(near_ref, near_out_ref, sent)
    fill_z([far_q_ref, near_q_ref], [], matrix(m_ref, OWN_ADJOINT), None, None, far_ref, near_ref,
           after=lambda at: copies[at].start())
    for copy in copies.values():
        copy.wait()


def adjoint_far_kernel(far_in_ref, *refs):
    *sib_refs, m_ref, unspread_ref, note_ref, log_ref, far_ref = refs
    add_sib(sib_refs, matrix(m_ref, SIB_ADJOINT), unspread_ref, far_in_ref, far_ref)
    to_log(lambda p: far_ref[p], far_ref.shape[0], m_ref, log_ref)
    for j in range(log_ref.shape[0] if log_ref.shape[1] > far_ref.shape[0] else 0):
        log_ref[j, far_ref.shape[0]] = note_ref[...]


def adjoint_near_kernel(near_in_ref, ext_ref, m_ref, unspread_ref, log_ref, near_ref, sum_ref, arrived):
    copy = pltpu.make_async_copy(near_in_ref, near_ref, arrived)
    copy.start()
    ext_z(ext_ref, matrix(m_ref, EXT_ADJOINT), unspread_ref, sum_ref)
    copy.wait()
    to_log(lambda p: near_ref[p] + sum_ref[p], sum_ref.shape[0], m_ref, log_ref)


def rows_kernel(at, view_ref, volume_ref, _, far_ref, near_ref, arrived):
    core, first = view_ref[0], pl.multiple_of(view_ref[1] * far_ref.shape[1], far_ref.shape[1])
    copies = []
    for i, ref in enumerate((far_ref, near_ref)):
        planes = jnp.where(core == 0, at[i][0], at[i][1])
        source = volume_ref.at[pl.ds(planes, ref.shape[0]), pl.ds(first, ref.shape[1]), :]
        copies.append(pltpu.make_async_copy(source, ref, arrived.at[i]))
    for copy in copies:
        copy.start()
    for copy in copies:
        copy.wait()


def assemble_kernel(blocks_ref, out_ref):
    depth, rows, ny = out_ref.shape
    for z in range(depth):
        exponent = blocks_ref[0, depth, z % rows:z % rows + 1, :]
        half = exponent[:, :ny // 2] if z < rows else exponent[:, ny // 2:]
        out_ref[z] = blocks_ref[0, z] * jnp.exp2(jnp.concatenate([half, half], axis=1) - 15.0)


def assemble(blocks, depth):
    views, planes, rows, ny = blocks.shape
    return pl.pallas_call(
        assemble_kernel,
        grid=(views,),
        out_shape=jax.ShapeDtypeStruct((depth, views * rows, ny), F32),
        in_specs=[pl.BlockSpec((1, planes, rows, ny), lambda j: (j, 0, 0, 0))],
        out_specs=pl.BlockSpec((depth, rows, ny), lambda j: (0, j, 0)),
        compiler_params=pltpu.CompilerParams(vmem_limit_bytes=20 * 1024 * 1024),
        cost_estimate=LIGHT,
    )(blocks)


def to_other_chip(planes):
    count = lax.axis_size("gz")
    pairs = [(i, i + 1) for i in range(1, count - 1, 2)]
    return lax.ppermute(planes, "gz", pairs + [(b, a) for a, b in pairs])


def to_sibling(planes):
    count = lax.axis_size("gz")
    return lax.ppermute(planes, "gz", [(i, i ^ 1) for i in range(count)])


def to_views(blocks):
    return lax.all_to_all(blocks, "view", 0, 0)


def sum_over_x(log_blocks):
    views = lax.axis_size("view")
    groups = [list(range(z, views, 2)) for z in range(2)]
    blocks = log_blocks.reshape((views // 2, 2) + log_blocks.shape[1:])
    return lax.all_to_all(blocks, "view", 0, 0, axis_index_groups=groups)


def to_z_partner(block):
    return lax.ppermute(block, "view", [(i, i ^ 1) for i in range(lax.axis_size("view"))])


def band(kernel_row, out_pos, in_pos):
    tap_index = in_pos[None, :] - out_pos[:, None] + RADIUS
    one_hot = (tap_index[:, :, None] == jnp.arange(TAPS, dtype=jnp.int32)[None, None, :]).astype(F32)
    return jnp.sum(one_hot * kernel_row[None, None, :], axis=2)


def gather_result(piece):
    views = lax.axis_size("view")
    depth, rows, ny = piece.shape
    exponent = jnp.maximum(jnp.ceil(jnp.log2(jnp.max(piece, axis=(1, 2)))), -100.0)
    scaled = piece * jnp.exp2(15.0 - exponent)[:, None, None]
    note = jnp.broadcast_to(exponent.reshape(depth // rows, rows, 1), (depth // rows, rows, ny * rows // depth))
    note = jnp.concatenate(list(note), axis=1)[None]
    wire = jnp.concatenate([scaled, note], axis=0).astype(jnp.float16)
    return assemble(to_views(jnp.broadcast_to(wire[None], (views,) + wire.shape)).astype(F32), depth)


def per_device(views_data, psf, start):
    kernels = psf[0] / jnp.sum(psf[0], axis=1, keepdims=True)
    recorded = views_data[0]
    depth, nx, ny = recorded.shape
    views = lax.axis_size("view")
    v = lax.axis_index("view")
    core = lax.axis_index("gz") % 2
    z_lo = v % 2
    rows = nx // views
    n_near, n_far = RADIUS, depth - RADIUS
    spread, unspread = jnp.asarray(SPREAD), jnp.asarray(UNSPREAD)

    near_at, far_at = (depth - n_near) * core, (depth - n_far) * (1 - core)

    def to_wire(planes):
        count = planes.shape[-2] // spread.shape[0]
        return (planes * jnp.concatenate([spread] * count, axis=0)).astype(BF16)

    core_at = core.reshape(1).astype(jnp.int32)
    far_planes, near_planes = (depth - n_far, 0), (0, depth - n_near)
    n_sib = n_far - n_far // 2
    far_shape, near_shape = (n_far, nx, ny), (n_near, nx, ny)
    by_rows = pltpu.SemaphoreType.DMA((nx // 16,))
    sib_shapes = [((n_sib, nx, ny), BF16), ((n_far - n_sib, nx, ny), BF16)]

    (wire_near,) = call(
        lambda *refs: wire_kernel(near_planes, *refs),
        [(near_shape, BF16)],
        [core_at, start],
        [pltpu.VMEM(near_shape, F32), pltpu.SemaphoreType.DMA((3,))],
        smem=1, hbm=(1,),
    )
    ext = to_other_chip(wire_near)
    (matrices,) = call(
        lambda *refs: band_kernel(n_near, n_far, *refs),
        [((MATRIX_ROWS, ny), F32)],
        [core_at, kernels, wire_near],
        smem=2, anywhere=(2,),
    )
    sib = call(
        lambda core_ref, volume_ref, _, *refs: wire_kernel(far_planes, core_ref, volume_ref, *refs),
        sib_shapes,
        [core_at, start, wire_near],
        [pltpu.VMEM(far_shape, F32), pltpu.SemaphoreType.DMA((3,))],
        smem=1, anywhere=(2,), hbm=(1,),
    )
    sib = [to_sibling(wire) for wire in sib]

    quotient_far, wire_far, partly = call(
        lambda *refs: first_far_kernel(far_planes, *refs),
        [(far_shape, F32), (far_shape, BF16), (near_shape, F32)],
        [core_at, start, *sib, matrices, unspread, recorded, spread],
        [pltpu.VMEM(far_shape, F32), pltpu.VMEM(far_shape, BF16), pltpu.SemaphoreType.DMA, pltpu.VMEM(start.shape, F32), by_rows],
        smem=1, hbm=(1, 6),
    )
    sib = [to_sibling(wire_far)]
    quotient_near, wire_near = call(
        lambda *refs: first_near_kernel(near_planes, *refs),
        [(near_shape, F32), (near_shape, BF16)],
        [core_at, partly, ext, matrices, unspread, recorded, spread],
        [pltpu.VMEM(near_shape, F32)],
        smem=1, cost=HEAVY,
    )
    ext = to_other_chip(wire_near)

    count = jnp.arange(depth, dtype=jnp.int32)
    out_z = jnp.where(count < n_far, far_at + count, near_at + count - n_far)
    sib_z = count[:n_far] + jnp.where(core == 0, depth, -n_far)
    ext_z = count[:n_near] + jnp.where(core == 0, -n_near, depth)

    high = kernels[2].astype(jnp.float16).astype(F32)
    low = ((kernels[2] - high) * 2048.0).astype(jnp.float16).astype(F32)
    note = jnp.pad(jnp.stack([high, low]), ((0, rows - 2), (0, ny - TAPS)))

    for iteration in range(ITERS):
        extra = 1 if iteration == 0 else 0
        far_own, partly = call(
            adjoint_own_kernel,
            [(far_shape, F32), (near_shape, F32)],
            [quotient_far, quotient_near, matrices],
            [pltpu.VMEM(near_shape, F32), by_rows],
            hbm_out=(1,),
        )
        (log_far,) = call(
            adjoint_far_kernel,
            [((views, n_far + extra, rows, ny), F32)],
            [far_own, *sib, matrices, unspread, note],
            [pltpu.VMEM(far_shape, F32)],
        )
        got = sum_over_x(log_far.astype(jnp.float16))

        (log_near,) = call(
            adjoint_near_kernel,
            [((views, n_near, rows, ny), F32)],
            [partly, ext, matrices, unspread],
            [pltpu.VMEM(near_shape, F32), pltpu.VMEM(near_shape, F32), pltpu.SemaphoreType.DMA],
            hbm=(0,), cost=HEAVY,
        )
        log_near, got = lax.optimization_barrier((log_near.astype(jnp.float16), got))
        sums = jnp.sum(got[:, :, :n_far].astype(F32), axis=0)
        own_sum, other = jnp.where(z_lo == 0, sums[0], sums[1]), jnp.where(z_lo == 0, sums[1], sums[0])
        other = other.astype(jnp.float16)
        if iteration == 0:
            mine = got[:, 0, n_far, :2, :TAPS].reshape(views, TAPS)
            mine_planes = jnp.pad(mine, ((0, rows - views), (0, ny - TAPS)))[None]
            other = to_z_partner(jnp.concatenate([other, mine_planes], axis=0))
            pair = [mine.astype(F32), other[n_far, :views, :TAPS].astype(F32)]
            pair = [t.reshape(views // 2, 2, TAPS) for t in pair]
            pair = [t[:, 0] + t[:, 1] / 2048.0 for t in pair]
            every_z = jnp.where(z_lo == 0, jnp.stack(pair, axis=1), jnp.stack(pair[::-1], axis=1)).reshape(views, TAPS)
            other = other[:n_far]
            piece_far, piece_near = call(
                lambda *refs: rows_kernel((far_planes, near_planes), *refs),
                [((n_far, rows, ny), F32), ((n_near, rows, ny), F32)],
                [jnp.stack([core, v]).astype(jnp.int32), start, own_sum],
                [pltpu.SemaphoreType.DMA((2,))],
                smem=1, anywhere=(2,), hbm=(1,),
            )
        else:
            other = to_z_partner(other)
        piece_far = piece_far * jnp.exp((own_sum + other.astype(F32)) / views)
        piece_near = piece_near * jnp.exp(jnp.sum(to_views(log_near).astype(F32), axis=0) / views)

        if iteration < ITERS - 1:
            wire_near = to_wire(piece_near)
            ext = to_other_chip(wire_near)
            piece_far, every_z, _ = lax.optimization_barrier((piece_far, every_z, wire_near))
            sib = to_sibling(to_wire(piece_far)).astype(F32) * unspread
            to_all = lambda planes, out, into: jnp.einsum(
                "zxy,voz->voxy", planes, jax.vmap(lambda row: band(row, out, into))(every_z), precision=lax.Precision.HIGH
            )
            planes = jnp.concatenate([piece_far, piece_near, sib, ext.astype(F32) * unspread], axis=0)
            blocks = to_wire(to_all(planes, out_z, jnp.concatenate([out_z, sib_z, ext_z])))
            blocks = to_views(blocks)
            quotient_near, wire_near = call(
                lambda *refs: block_kernel(n_far, near_planes, *refs),
                [(near_shape, F32), (near_shape, BF16)],
                [core_at, core_at, blocks, matrices, unspread, recorded, spread],
                smem=2, cost=HEAVY,
            )
            ext = to_other_chip(wire_near)
            quotient_far, wire_a, wire_b = call(
                lambda *refs: block_kernel(0, far_planes, *refs),
                [(far_shape, F32)] + sib_shapes,
                [core_at, wire_near, blocks, matrices, unspread, recorded, spread],
                smem=1, anywhere=(1,),
            )
            sib = [to_sibling(wire_a), to_sibling(wire_b)]

    both = jnp.concatenate([piece_near, piece_far, piece_near], axis=0)
    return gather_result(lax.dynamic_slice_in_dim(both, n_near * core, depth, axis=0))


def solution(mesh):
    in_specs = (P("view", "gz", None, None), P("view", None, None), P("gz", None, None))
    out_specs = P("gz", None, None)
    return jax.shard_map(
        per_device, mesh=mesh, in_specs=in_specs, out_specs=out_specs, check_vma=False
    )
```

```python
import math

import jax
import jax.numpy as jnp
import numpy as np
from jax import lax
from jax.experimental import pallas as pl
from jax.experimental.pallas import tpu as pltpu
from jax.sharding import PartitionSpec as P

RADIUS = 15
TAPS = 31
ITERS = 2
F32, BF16 = jnp.float32, jnp.bfloat16
GROUP = 8

ROW_STEP, COLUMN_STEP = 49471, 37345
_PHASE = np.arange(16)[:, None] * ROW_STEP + np.arange(256)[None, :] * COLUMN_STEP
SPREAD = (1.0 + (_PHASE % 65536) / 65536.0).astype(np.float32)
UNSPREAD = (1.0 / SPREAD.astype(np.float64)).astype(np.float32)


def spread_pattern(shape):
    row, column = lax.broadcasted_iota(jnp.int32, shape, 0), lax.broadcasted_iota(jnp.int32, shape, 1)
    return 1.0 + ((row * ROW_STEP + column * COLUMN_STEP) % 65536).astype(F32) / 65536.0


LIGHT = pl.CostEstimate(flops=1000, bytes_accessed=1000, transcendentals=0)
HEAVY = pl.CostEstimate(flops=6 * 10**10, bytes_accessed=2 * 10**8, transcendentals=0)


def call(kernel, outs, args, scratch=(), smem=0, anywhere=(), hbm=(), hbm_out=(), cost=LIGHT):
    held = sum(math.prod(a.shape) * jnp.dtype(a.dtype).itemsize for a in scratch if getattr(a, "memory_space", None) == pltpu.VMEM)
    anywhere = set(anywhere) | set(hbm)
    specs = [pl.BlockSpec(memory_space=pltpu.SMEM)] * smem
    specs += [pl.BlockSpec(memory_space=pl.ANY if i in anywhere else pltpu.VMEM) for i in range(smem, len(args))]
    args = [pltpu.with_memory_space_constraint(a, pltpu.HBM) if i in hbm else a for i, a in enumerate(args)]
    return pl.pallas_call(
        kernel,
        out_shape=[
            (pltpu.HBM if i in hbm_out else jax.ShapeDtypeStruct)(shape, dtype) for i, (shape, dtype) in enumerate(outs)
        ],
        in_specs=specs,
        out_specs=[
            pl.BlockSpec(memory_space=pl.ANY if i in hbm_out else pltpu.VMEM) for i in range(len(outs))
        ],
        scratch_shapes=list(scratch),
        compiler_params=pltpu.CompilerParams(vmem_limit_bytes=held + 3 * 1024 * 1024),
        cost_estimate=cost,
    )(*args)


def split(a):
    high = a.astype(BF16)
    return high, (a - high.astype(F32)).astype(BF16)


def mul(a, b):
    return jnp.dot(a, b, preferred_element_type=F32)


def mul3(a, b):
    return mul(a[0], b[0]) + mul(a[0], b[1]) + mul(a[1], b[0])


def tile_rows(pattern, rows):
    return jnp.concatenate([pattern] * (rows // pattern.shape[0]), axis=0)


X_ADJOINT, EXT_ADJOINT, Y_ADJOINT = (0, 0, 128, 128), (0, 128, 120, 128), (128, 0, 256, 256)
KEPT_ROWS = 384
Y_FORWARD = (0, 0, 256, 256)
OWN_FORWARD, OWN_ADJOINT = (256, 0, 256, 256), (512, 0, 256, 256)
SIB_FORWARD, SIB_ADJOINT = (768, 0, 136, 144), (904, 0, 136, 144)
X_FORWARD, EXT_FORWARD = (1040, 0, 128, 128), (1040, 128, 120, 128)
OTHER_ROWS = 1168


def matrix(ref, where):
    row, column, rows, columns = where
    return split(ref[row:row + rows, column:column + columns])


def band_kernel(n_near, n_far, kept, core_ref, taps_ref, _, out_ref):
    depth = n_near + n_far
    core = core_ref[0]
    near_at, far_at = (depth - n_near) * core, (depth - n_far) * (1 - core)
    natural = lambda i: i
    ordered = lambda i: jnp.where(i < n_far, far_at + i, near_at + i - n_far)
    near = lambda i: near_at + i
    ext = lambda i: i + jnp.where(core == 0, -n_near, depth)
    sib = lambda i: jnp.where(i < n_far, i + jnp.where(core == 0, depth, -n_far), 4 * depth)
    plans = [
        (X_ADJOINT, 0, natural, natural, -1, 1), (EXT_ADJOINT, 2, near, ext, -1, GROUP), (Y_ADJOINT, 1, natural, natural, 1, 1),
    ] if kept else [
        (Y_FORWARD, 1, natural, natural, -1, 1),
        (OWN_FORWARD, 2, ordered, natural, 1, GROUP), (OWN_ADJOINT, 2, ordered, ordered, -1, GROUP),
        (SIB_FORWARD, 2, ordered, sib, 1, GROUP), (SIB_ADJOINT, 2, ordered, sib, -1, GROUP),
        (X_FORWARD, 0, natural, natural, 1, 1), (EXT_FORWARD, 2, near, ext, 1, GROUP),
    ]
    for (at, column_at, rows, columns), axis, out_pos, in_pos, direction, repeat in plans:
        columns = -(-columns // 128) * 128
        row = lax.broadcasted_iota(jnp.int32, (rows, columns), 0)
        column = lax.broadcasted_iota(jnp.int32, (rows, columns), 1)
        tap = direction * (in_pos(column // repeat) - out_pos(row // repeat)) + RADIUS
        if repeat > 1:
            tap = jnp.where(row % repeat == column % repeat, tap, -1)
        total = jnp.zeros((rows, columns), F32)
        for k in range(TAPS):
            total = total + jnp.where(tap == k, taps_ref[axis, k], 0.0)
        out_ref[at:at + rows, column_at:column_at + columns] = total


def wire_kernel(at, core_ref, volume_ref, *refs):
    *wire_refs, buffer, arrived = refs
    first = jnp.where(core_ref[0] == 0, at[0], at[1])
    count, step = buffer.shape[0], -(-buffer.shape[0] // arrived.shape[0])
    parts = [slice(p, min(p + step, count)) for p in range(0, count, step)]
    copies = [
        pltpu.make_async_copy(volume_ref.at[pl.ds(first + r.start, r.stop - r.start)], buffer.at[r], arrived.at[i])
        for i, r in enumerate(parts)
    ]
    for copy in copies:
        copy.start()
    pattern = tile_rows(spread_pattern((16, buffer.shape[2])), buffer.shape[1])
    done = 0
    for wire_ref in wire_refs:
        for p in range(wire_ref.shape[0]):
            if done % step == 0:
                copies[done // step].wait()
            wire_ref[p] = (buffer[done] * pattern).astype(BF16)
            done += 1


def blur_rows(planes, mx, my):
    return mul3(split(mul3(mx, split(planes))), my)


def own_rows_z(own, wo):
    return mul3(wo, split(own))


def sib_rows_z(sib_refs, at, half, ws, unspread):
    sib = [r[:, pl.ds(at, 16), :].astype(F32)[:, half * GROUP:(half + 1) * GROUP] for r in sib_refs]
    sib = [a.reshape(a.shape[0] * GROUP, -1) for a in sib]
    rest = ws[0].shape[1] - sum(a.shape[0] for a in sib)
    sib = jnp.concatenate(sib + [jnp.zeros((rest, sib[0].shape[1]), F32)], axis=0).astype(BF16)
    other = mul(ws[0], sib) + mul(ws[1], sib)
    return other * tile_rows(unspread[half * GROUP:(half + 1) * GROUP], other.shape[0])


def fill_z(own_refs, sib_refs, wo, ws, unspread_ref, far_ref, near_ref, spread_ref=None, before=None):
    nx, ny = far_ref.shape[1:]
    cut = far_ref.shape[0] * GROUP
    for at in range(0, nx, 16):
        if before:
            before(at)
        near = []
        for half in range(2):
            here = slice(at + half * GROUP, at + (half + 1) * GROUP)
            own = jnp.concatenate([r[:, here, :].reshape(r.shape[0] * GROUP, ny) for r in own_refs], axis=0)
            out = own_rows_z(own, wo)
            far = out[:cut]
            if sib_refs:
                far = far + sib_rows_z(sib_refs, at, half, ws, unspread_ref[...])
            far_ref[:, here, :] = far.reshape(far_ref.shape[0], GROUP, ny)
            near.append(out[cut:].reshape(near_ref.shape[0], GROUP, ny))
        near = jnp.concatenate(near, axis=1)
        if spread_ref is not None:
            near = (near * spread_ref[...][None]).astype(BF16)
        near_ref[:, at:at + 16, :] = near


def add_sib(sib_refs, ws, unspread_ref, far_in_ref, far_ref):
    n, nx, ny = far_ref.shape

    def step(g, _):
        at = pl.multiple_of(g * 16, 16)
        for half in range(2):
            here = pl.ds(pl.multiple_of(at + half * GROUP, GROUP), GROUP)
            other = sib_rows_z(sib_refs, at, half, ws, unspread_ref[...])
            far_ref[:, here, :] = far_in_ref[:, here, :] + other.reshape(n, GROUP, ny)
        return 0

    lax.fori_loop(0, nx // 16, step, 0, unroll=True)


def copies_by_rows(source, target, done):
    rows = [slice(at, at + 16) for at in range(0, source.shape[1], 16)]
    return {r.start: pltpu.make_async_copy(source.at[:, r, :], target.at[:, r, :], done.at[i]) for i, r in enumerate(rows)}


def planes_from(first, core_ref, ref):
    at = jnp.where(core_ref[0] == 0, first[0], first[1])
    return lambda p: ref[at + p]


def ext_z(ext_ref, we, out_ref):
    n, nx, ny = out_ref.shape
    for at in range(0, nx, 2 * GROUP):
        block = ext_ref[:, at:at + 2 * GROUP, :].astype(F32)
        for half in range(2):
            ext = block[:, half * GROUP:(half + 1) * GROUP].reshape(n * GROUP, ny)
            ext = jnp.concatenate([ext, jnp.zeros((we[0].shape[1] - n * GROUP, ny), F32)], axis=0).astype(BF16)
            other = mul(we[0], ext) + mul(we[1], ext)
            here = slice(at + half * GROUP, at + (half + 1) * GROUP)
            out_ref[:, here, :] = other.reshape(n, GROUP, ny)


def to_quotient(load, recorded, more_ref, spread_ref, quotient_ref, wire_refs):
    mx, my = matrix(more_ref, X_FORWARD), matrix(more_ref, Y_FORWARD)
    pattern = tile_rows(spread_ref[...], quotient_ref.shape[1])
    for p in range(quotient_ref.shape[0]):
        quotient = recorded(p).astype(F32) / blur_rows(load(p), mx, my)
        quotient_ref[p] = quotient
        wire, at = (wire_refs[0], p) if p < wire_refs[0].shape[0] else (wire_refs[1], p - wire_refs[0].shape[0])
        wire[at] = (quotient * pattern).astype(BF16)


def to_log(load, count, m_ref, log_ref):
    mx, my = matrix(m_ref, X_ADJOINT), matrix(m_ref, Y_ADJOINT)
    views, _, rows, ny = log_ref.shape
    for p in range(count):
        log_ref[:, p] = jnp.log(blur_rows(load(p), mx, my)).reshape(views, rows, ny)


def first_far_kernel(first, core_ref, start_ref, sib_a_ref, sib_b_ref, more_ref, unspread_ref, recorded_ref, spread_ref,
                     quotient_ref, wire_ref, near_ref, far_ref, recorded, recorded_done, start, start_done):
    copies = copies_by_rows(start_ref, start, start_done)
    for copy in copies.values():
        copy.start()
    planes = pl.ds(jnp.where(core_ref[0] == 0, first[0], first[1]), recorded.shape[0])
    copy = pltpu.make_async_copy(recorded_ref.at[planes], recorded, recorded_done)
    copy.start()
    own, sib = matrix(more_ref, OWN_FORWARD), matrix(more_ref, SIB_FORWARD)
    fill_z([start], [sib_a_ref, sib_b_ref], own, sib, unspread_ref, far_ref, near_ref, before=lambda at: copies[at].wait())
    copy.wait()
    to_quotient(lambda p: far_ref[p], lambda p: recorded[p], more_ref, spread_ref, quotient_ref, [wire_ref])


def first_near_kernel(first, core_ref, near_ref, ext_ref, more_ref, unspread_ref, recorded_ref, spread_ref,
                      quotient_ref, wire_ref, sum_ref):
    ext_z(ext_ref, matrix(more_ref, EXT_FORWARD), sum_ref)
    recorded = planes_from(first, core_ref, recorded_ref)
    pattern = tile_rows(unspread_ref[...], sum_ref.shape[1])
    to_quotient(lambda p: near_ref[p] + sum_ref[p] * pattern, recorded, more_ref, spread_ref, quotient_ref, [wire_ref])


def block_kernel(block, first, core_ref, _, blocks_ref, more_ref, unspread_ref, recorded_ref, spread_ref, quotient_ref, *wire_refs):
    views, _, rows, ny = blocks_ref.shape
    pattern = tile_rows(unspread_ref[...], views * rows)

    def load(p):
        return blocks_ref[:, block + p].reshape(views * rows, ny).astype(F32) * pattern

    to_quotient(load, planes_from(first, core_ref, recorded_ref), more_ref, spread_ref, quotient_ref, wire_refs)


def adjoint_own_kernel(far_q_ref, near_q_ref, more_ref, spread_ref, far_ref, near_ref):
    fill_z([far_q_ref, near_q_ref], [], matrix(more_ref, OWN_ADJOINT), None, None, far_ref, near_ref, spread_ref)


def adjoint_far_kernel(far_in_ref, *refs):
    *sib_refs, m_ref, more_ref, unspread_ref, note_ref, log_ref, far_ref = refs
    add_sib(sib_refs, matrix(more_ref, SIB_ADJOINT), unspread_ref, far_in_ref, far_ref)
    to_log(lambda p: far_ref[p], far_ref.shape[0], m_ref, log_ref)
    for j in range(log_ref.shape[0] if log_ref.shape[1] > far_ref.shape[0] else 0):
        log_ref[j, far_ref.shape[0]] = note_ref[...]


def adjoint_near_kernel(near_ref, ext_ref, m_ref, unspread_ref, log_ref, sum_ref):
    ext_z(ext_ref, matrix(m_ref, EXT_ADJOINT), sum_ref)
    pattern = tile_rows(unspread_ref[...], sum_ref.shape[1])
    to_log(lambda p: (near_ref[p].astype(F32) + sum_ref[p]) * pattern, sum_ref.shape[0], m_ref, log_ref)


def rows_kernel(at, view_ref, volume_ref, _, __, far_ref, near_ref, arrived):
    core, first = view_ref[0], pl.multiple_of(view_ref[1] * far_ref.shape[1], far_ref.shape[1])
    copies = []
    for i, ref in enumerate((far_ref, near_ref)):
        planes = jnp.where(core == 0, at[i][0], at[i][1])
        source = volume_ref.at[pl.ds(planes, ref.shape[0]), pl.ds(first, ref.shape[1]), :]
        copies.append(pltpu.make_async_copy(source, ref, arrived.at[i]))
    for copy in copies:
        copy.start()
    for copy in copies:
        copy.wait()


def assemble_kernel(blocks_ref, out_ref, buffer, sent):
    depth, _, ny = out_ref.shape
    views, _, rows, _ = blocks_ref.shape
    step = depth // sent.shape[0]
    copies = []
    for z in range(depth):
        for j in range(views):
            exponent = blocks_ref[j, depth, z % rows:z % rows + 1, :]
            half = exponent[:, :ny // 2] if z < rows else exponent[:, ny // 2:]
            scale = jnp.exp2(jnp.concatenate([half, half], axis=1) - 15.0)
            buffer[z, j * rows:(j + 1) * rows] = blocks_ref[j, z] * scale
        if z % step == step - 1:
            part = slice(z + 1 - step, z + 1)
            copies.append(pltpu.make_async_copy(buffer.at[part], out_ref.at[part], sent.at[len(copies)]))
            copies[-1].start()
    for copy in copies:
        copy.wait()


def assemble(blocks, depth):
    views, _, rows, ny = blocks.shape
    shape = (depth, views * rows, ny)
    (out,) = call(assemble_kernel, [(shape, F32)], [blocks], [pltpu.VMEM(shape, F32), pltpu.SemaphoreType.DMA((8,))], hbm_out=(0,))
    return out


def to_other_chip(planes):
    count = lax.axis_size("gz")
    pairs = [(i, i + 1) for i in range(1, count - 1, 2)]
    return lax.ppermute(planes, "gz", pairs + [(b, a) for a, b in pairs])


def to_sibling(planes):
    count = lax.axis_size("gz")
    return lax.ppermute(planes, "gz", [(i, i ^ 1) for i in range(count)])


def to_views(blocks):
    return lax.all_to_all(blocks, "view", 0, 0)


def sum_over_x(log_blocks):
    views = lax.axis_size("view")
    groups = [list(range(z, views, 2)) for z in range(2)]
    blocks = log_blocks.reshape((views // 2, 2) + log_blocks.shape[1:])
    return lax.all_to_all(blocks, "view", 0, 0, axis_index_groups=groups)


def to_z_partner(block):
    return lax.ppermute(block, "view", [(i, i ^ 1) for i in range(lax.axis_size("view"))])


def band(kernel_row, out_pos, in_pos):
    tap_index = in_pos[None, :] - out_pos[:, None] + RADIUS
    one_hot = (tap_index[:, :, None] == jnp.arange(TAPS, dtype=jnp.int32)[None, None, :]).astype(F32)
    return jnp.sum(one_hot * kernel_row[None, None, :], axis=2)


def gather_result(piece):
    views = lax.axis_size("view")
    depth, rows, ny = piece.shape
    exponent = jnp.maximum(jnp.ceil(jnp.log2(jnp.max(piece, axis=(1, 2)))), -100.0)
    scaled = piece * jnp.exp2(15.0 - exponent)[:, None, None]
    note = jnp.broadcast_to(exponent.reshape(depth // rows, rows, 1), (depth // rows, rows, ny * rows // depth))
    note = jnp.concatenate(list(note), axis=1)[None]
    wire = jnp.concatenate([scaled, note], axis=0).astype(jnp.float16)
    return assemble(to_views(jnp.broadcast_to(wire[None], (views,) + wire.shape)).astype(F32), depth)


def per_device(views_data, psf, start):
    kernels = psf[0] / jnp.sum(psf[0], axis=1, keepdims=True)
    recorded = views_data[0]
    depth, nx, ny = recorded.shape
    views = lax.axis_size("view")
    v = lax.axis_index("view")
    core = lax.axis_index("gz") % 2
    z_lo = v % 2
    rows = nx // views
    n_near, n_far = RADIUS, depth - RADIUS
    spread, unspread = jnp.asarray(SPREAD), jnp.asarray(UNSPREAD)

    near_at, far_at = (depth - n_near) * core, (depth - n_far) * (1 - core)

    def to_wire(planes):
        count = planes.shape[-2] // spread.shape[0]
        return (planes * jnp.concatenate([spread] * count, axis=0)).astype(BF16)

    core_at = core.reshape(1).astype(jnp.int32)
    far_planes, near_planes = (depth - n_far, 0), (0, depth - n_near)
    n_sib = n_far - n_far // 2
    far_shape, near_shape = (n_far, nx, ny), (n_near, nx, ny)
    by_rows = pltpu.SemaphoreType.DMA((nx // 16,))
    sib_shapes = [((n_sib, nx, ny), BF16), ((n_far - n_sib, nx, ny), BF16)]

    (wire_near,) = call(
        lambda *refs: wire_kernel(near_planes, *refs),
        [(near_shape, BF16)],
        [core_at, start],
        [pltpu.VMEM(near_shape, F32), pltpu.SemaphoreType.DMA((3,))],
        smem=1, hbm=(1,),
    )
    ext = to_other_chip(wire_near)

    def matrices(rows, after):
        return call(
            lambda *refs: band_kernel(n_near, n_far, rows == KEPT_ROWS, *refs),
            [((rows, ny), F32)],
            [core_at, kernels, after],
            smem=2, anywhere=(2,),
        )[0]

    kept, more = matrices(KEPT_ROWS, wire_near), matrices(OTHER_ROWS, wire_near)
    sib = call(
        lambda core_ref, volume_ref, _, *refs: wire_kernel(far_planes, core_ref, volume_ref, *refs),
        sib_shapes,
        [core_at, start, wire_near],
        [pltpu.VMEM(far_shape, F32), pltpu.SemaphoreType.DMA((3,))],
        smem=1, anywhere=(2,), hbm=(1,),
    )
    sib = [to_sibling(wire) for wire in sib]

    quotient_far, wire_far, partly = call(
        lambda *refs: first_far_kernel(far_planes, *refs),
        [(far_shape, F32), (far_shape, BF16), (near_shape, F32)],
        [core_at, start, *sib, more, unspread, recorded, spread],
        [pltpu.VMEM(far_shape, F32), pltpu.VMEM(far_shape, BF16), pltpu.SemaphoreType.DMA, pltpu.VMEM(start.shape, F32), by_rows],
        smem=1, hbm=(1, 6),
    )
    sib = [to_sibling(wire_far)]
    quotient_near, wire_near = call(
        lambda *refs: first_near_kernel(near_planes, *refs),
        [(near_shape, F32), (near_shape, BF16)],
        [core_at, partly, ext, more, unspread, recorded, spread],
        [pltpu.VMEM(near_shape, F32)],
        smem=1, cost=HEAVY,
    )
    ext = to_other_chip(wire_near)

    count = jnp.arange(depth, dtype=jnp.int32)
    out_z = jnp.where(count < n_far, far_at + count, near_at + count - n_far)
    sib_z = count[:n_far] + jnp.where(core == 0, depth, -n_far)
    ext_z = count[:n_near] + jnp.where(core == 0, -n_near, depth)

    high = kernels[2].astype(jnp.float16).astype(F32)
    low = ((kernels[2] - high) * 2048.0).astype(jnp.float16).astype(F32)
    note = jnp.pad(jnp.stack([high, low]), ((0, rows - 2), (0, ny - TAPS)))

    for iteration in range(ITERS):
        extra = 1 if iteration == 0 else 0
        far_own, partly = call(
            adjoint_own_kernel,
            [(far_shape, F32), (near_shape, BF16)],
            [quotient_far, quotient_near, more, spread],
        )
        (log_far,) = call(
            adjoint_far_kernel,
            [((views, n_far + extra, rows, ny), F32)],
            [far_own, *sib, kept, more, unspread, note],
            [pltpu.VMEM(far_shape, F32)],
        )
        got = sum_over_x(log_far.astype(jnp.float16))

        (log_near,) = call(
            adjoint_near_kernel,
            [((views, n_near, rows, ny), F32)],
            [partly, ext, kept, unspread],
            [pltpu.VMEM(near_shape, F32)],
            cost=HEAVY,
        )
        log_near, got = lax.optimization_barrier((log_near.astype(jnp.float16), got))
        sums = jnp.sum(got[:, :, :n_far].astype(F32), axis=0)
        own_sum, other = jnp.where(z_lo == 0, sums[0], sums[1]), jnp.where(z_lo == 0, sums[1], sums[0])
        other = other.astype(jnp.float16)
        if iteration == 0:
            mine = got[:, 0, n_far, :2, :TAPS].reshape(views, TAPS)
            mine_planes = jnp.pad(mine, ((0, rows - views), (0, ny - TAPS)))[None]
            other = to_z_partner(jnp.concatenate([other, mine_planes], axis=0))
            pair = [mine.astype(F32), other[n_far, :views, :TAPS].astype(F32)]
            pair = [t.reshape(views // 2, 2, TAPS) for t in pair]
            pair = [t[:, 0] + t[:, 1] / 2048.0 for t in pair]
            every_z = jnp.where(z_lo == 0, jnp.stack(pair, axis=1), jnp.stack(pair[::-1], axis=1)).reshape(views, TAPS)
            other = other[:n_far]
            more = matrices(OTHER_ROWS, own_sum)
            piece_far, piece_near = call(
                lambda *refs: rows_kernel((far_planes, near_planes), *refs),
                [((n_far, rows, ny), F32), ((n_near, rows, ny), F32)],
                [jnp.stack([core, v]).astype(jnp.int32), start, own_sum, more],
                [pltpu.SemaphoreType.DMA((2,))],
                smem=1, anywhere=(2, 3), hbm=(1,),
            )
        else:
            other = to_z_partner(other)
        piece_far = piece_far * jnp.exp((own_sum + other.astype(F32)) / views)
        piece_near = piece_near * jnp.exp(jnp.sum(to_views(log_near).astype(F32), axis=0) / views)

        if iteration < ITERS - 1:
            wire_near = to_wire(piece_near)
            ext = to_other_chip(wire_near)
            piece_far, every_z, _ = lax.optimization_barrier((piece_far, every_z, wire_near))
            sib = to_sibling(to_wire(piece_far)).astype(F32) * unspread
            to_all = lambda planes, out, into: jnp.einsum(
                "zxy,voz->voxy", planes, jax.vmap(lambda row: band(row, out, into))(every_z), precision=lax.Precision.HIGH
            )
            planes = jnp.concatenate([piece_far, piece_near, sib, ext.astype(F32) * unspread], axis=0)
            blocks = to_wire(to_all(planes, out_z, jnp.concatenate([out_z, sib_z, ext_z])))
            blocks = to_views(blocks)
            quotient_near, wire_near = call(
                lambda *refs: block_kernel(n_far, near_planes, *refs),
                [(near_shape, F32), (near_shape, BF16)],
                [core_at, core_at, blocks, more, unspread, recorded, spread],
                smem=2, cost=HEAVY,
            )
            ext = to_other_chip(wire_near)
            quotient_far, wire_a, wire_b = call(
                lambda *refs: block_kernel(0, far_planes, *refs),
                [(far_shape, F32)] + sib_shapes,
                [core_at, wire_near, blocks, more, unspread, recorded, spread],
                smem=1, anywhere=(1,),
            )
            sib = [to_sibling(wire_a), to_sibling(wire_b)]

    both = jnp.concatenate([piece_near, piece_far, piece_near], axis=0)
    return gather_result(lax.dynamic_slice_in_dim(both, n_near * core, depth, axis=0))


def solution(mesh):
    in_specs = (P("view", "gz", None, None), P("view", None, None), P("gz", None, None))
    out_specs = P("gz", None, None)
    return jax.shard_map(
        per_device, mesh=mesh, in_specs=in_specs, out_specs=out_specs, check_vma=False
    )
```

```python
import math

import jax
import jax.numpy as jnp
import numpy as np
from jax import lax
from jax.experimental import pallas as pl
from jax.experimental.pallas import tpu as pltpu
from jax.sharding import PartitionSpec as P

RADIUS = 15
TAPS = 31
ITERS = 2
F32, BF16 = jnp.float32, jnp.bfloat16
GROUP = 8

ROW_STEP, COLUMN_STEP = 49471, 37345
_PHASE = np.arange(16)[:, None] * ROW_STEP + np.arange(256)[None, :] * COLUMN_STEP
SPREAD = (1.0 + (_PHASE % 65536) / 65536.0).astype(np.float32)
UNSPREAD = (1.0 / SPREAD.astype(np.float64)).astype(np.float32)


def spread_pattern(shape):
    row, column = lax.broadcasted_iota(jnp.int32, shape, 0), lax.broadcasted_iota(jnp.int32, shape, 1)
    return 1.0 + ((row * ROW_STEP + column * COLUMN_STEP) % 65536).astype(F32) / 65536.0


LIGHT = pl.CostEstimate(flops=1000, bytes_accessed=1000, transcendentals=0)
HEAVY = pl.CostEstimate(flops=6 * 10**10, bytes_accessed=2 * 10**8, transcendentals=0)


def call(kernel, outs, args, scratch=(), smem=0, anywhere=(), hbm=(), hbm_out=(), cost=LIGHT):
    held = sum(math.prod(a.shape) * jnp.dtype(a.dtype).itemsize for a in scratch if getattr(a, "memory_space", None) == pltpu.VMEM)
    anywhere = set(anywhere) | set(hbm)
    specs = [pl.BlockSpec(memory_space=pltpu.SMEM)] * smem
    specs += [pl.BlockSpec(memory_space=pl.ANY if i in anywhere else pltpu.VMEM) for i in range(smem, len(args))]
    args = [pltpu.with_memory_space_constraint(a, pltpu.HBM) if i in hbm else a for i, a in enumerate(args)]
    return pl.pallas_call(
        kernel,
        out_shape=[
            (pltpu.HBM if i in hbm_out else jax.ShapeDtypeStruct)(shape, dtype) for i, (shape, dtype) in enumerate(outs)
        ],
        in_specs=specs,
        out_specs=[
            pl.BlockSpec(memory_space=pl.ANY if i in hbm_out else pltpu.VMEM) for i in range(len(outs))
        ],
        scratch_shapes=list(scratch),
        compiler_params=pltpu.CompilerParams(vmem_limit_bytes=held + 3 * 1024 * 1024),
        cost_estimate=cost,
    )(*args)


def split(a):
    high = a.astype(BF16)
    return high, (a - high.astype(F32)).astype(BF16)


def mul(a, b):
    return jnp.dot(a, b, preferred_element_type=F32)


def mul3(a, b):
    return mul(a[0], b[0]) + mul(a[0], b[1]) + mul(a[1], b[0])


def mul2(a, b):
    return mul(jnp.concatenate(a, axis=1), jnp.concatenate([b, b], axis=0))


def tile_rows(pattern, rows):
    return jnp.concatenate([pattern] * (rows // pattern.shape[0]), axis=0)


X_ADJOINT, EXT_ADJOINT, Y_ADJOINT = (0, 0, 128, 128), (0, 128, 120, 128), (128, 0, 256, 256)
KEPT_ROWS = 384
Y_FORWARD = (0, 0, 256, 256)
OWN_FORWARD, OWN_ADJOINT = (256, 0, 256, 256), (512, 0, 256, 256)
SIB_FORWARD, SIB_ADJOINT = (768, 0, 136, 144), (904, 0, 136, 144)
X_FORWARD, EXT_FORWARD = (1040, 0, 128, 128), (1040, 128, 120, 128)
OTHER_ROWS = 1168


def matrix(ref, where):
    row, column, rows, columns = where
    return split(ref[row:row + rows, column:column + columns])


def band_kernel(n_near, n_far, kept, core_ref, taps_ref, _, out_ref):
    depth = n_near + n_far
    core = core_ref[0]
    near_at, far_at = (depth - n_near) * core, (depth - n_far) * (1 - core)
    natural = lambda i: i
    ordered = lambda i: jnp.where(i < n_far, far_at + i, near_at + i - n_far)
    near = lambda i: near_at + i
    ext = lambda i: i + jnp.where(core == 0, -n_near, depth)
    sib = lambda i: jnp.where(i < n_far, i + jnp.where(core == 0, depth, -n_far), 4 * depth)
    plans = [
        (X_ADJOINT, 0, natural, natural, -1, 1), (EXT_ADJOINT, 2, near, ext, -1, GROUP), (Y_ADJOINT, 1, natural, natural, 1, 1),
    ] if kept else [
        (Y_FORWARD, 1, natural, natural, -1, 1),
        (OWN_FORWARD, 2, ordered, natural, 1, GROUP), (OWN_ADJOINT, 2, ordered, ordered, -1, GROUP),
        (SIB_FORWARD, 2, ordered, sib, 1, GROUP), (SIB_ADJOINT, 2, ordered, sib, -1, GROUP),
        (X_FORWARD, 0, natural, natural, 1, 1), (EXT_FORWARD, 2, near, ext, 1, GROUP),
    ]
    for (at, column_at, rows, columns), axis, out_pos, in_pos, direction, repeat in plans:
        columns = -(-columns // 128) * 128
        row = lax.broadcasted_iota(jnp.int32, (rows, columns), 0)
        column = lax.broadcasted_iota(jnp.int32, (rows, columns), 1)
        tap = direction * (in_pos(column // repeat) - out_pos(row // repeat)) + RADIUS
        if repeat > 1:
            tap = jnp.where(row % repeat == column % repeat, tap, -1)
        total = jnp.zeros((rows, columns), F32)
        for k in range(TAPS):
            total = total + jnp.where(tap == k, taps_ref[axis, k], 0.0)
        out_ref[at:at + rows, column_at:column_at + columns] = total


def wire_kernel(at, core_ref, volume_ref, *refs):
    *wire_refs, buffer, arrived = refs
    first = jnp.where(core_ref[0] == 0, at[0], at[1])
    count, step = buffer.shape[0], -(-buffer.shape[0] // arrived.shape[0])
    parts = [slice(p, min(p + step, count)) for p in range(0, count, step)]
    copies = [
        pltpu.make_async_copy(volume_ref.at[pl.ds(first + r.start, r.stop - r.start)], buffer.at[r], arrived.at[i])
        for i, r in enumerate(parts)
    ]
    for copy in copies:
        copy.start()
    pattern = tile_rows(spread_pattern((16, buffer.shape[2])), buffer.shape[1])
    done = 0
    for wire_ref in wire_refs:
        for p in range(wire_ref.shape[0]):
            if done % step == 0:
                copies[done // step].wait()
            wire_ref[p] = (buffer[done] * pattern).astype(BF16)
            done += 1


def blur_rows(planes, mx, my):
    return mul3(split(mul3(mx, split(planes))), my)


def own_rows_z(own, wo):
    return mul3(wo, split(own))


def sib_rows_z(sib_refs, at, half, ws, unspread):
    sib = [r[:, pl.ds(at, 16), :].astype(F32)[:, half * GROUP:(half + 1) * GROUP] for r in sib_refs]
    sib = [a.reshape(a.shape[0] * GROUP, -1) for a in sib]
    rest = ws[0].shape[1] - sum(a.shape[0] for a in sib)
    sib = jnp.concatenate(sib + [jnp.zeros((rest, sib[0].shape[1]), F32)], axis=0).astype(BF16)
    other = mul(ws[0], sib) + mul(ws[1], sib)
    return other * tile_rows(unspread[half * GROUP:(half + 1) * GROUP], other.shape[0])


def fill_z(own_refs, sib_refs, wo, ws, unspread_ref, far_ref, near_ref, spread_ref=None, before=None):
    nx, ny = far_ref.shape[1:]
    cut = far_ref.shape[0] * GROUP
    for at in range(0, nx, 16):
        if before:
            before(at)
        near = []
        for half in range(2):
            here = slice(at + half * GROUP, at + (half + 1) * GROUP)
            own = jnp.concatenate([r[:, here, :].reshape(r.shape[0] * GROUP, ny) for r in own_refs], axis=0)
            out = own_rows_z(own, wo)
            far = out[:cut]
            if sib_refs:
                far = far + sib_rows_z(sib_refs, at, half, ws, unspread_ref[...])
            far_ref[:, here, :] = far.reshape(far_ref.shape[0], GROUP, ny)
            near.append(out[cut:].reshape(near_ref.shape[0], GROUP, ny))
        near = jnp.concatenate(near, axis=1)
        if spread_ref is not None:
            near = (near * spread_ref[...][None]).astype(BF16)
        near_ref[:, at:at + 16, :] = near


def add_sib(sib_refs, ws, unspread_ref, far_in_ref, far_ref):
    n, nx, ny = far_ref.shape

    def step(g, _):
        at = pl.multiple_of(g * 16, 16)
        for half in range(2):
            here = pl.ds(pl.multiple_of(at + half * GROUP, GROUP), GROUP)
            other = sib_rows_z(sib_refs, at, half, ws, unspread_ref[...])
            far_ref[:, here, :] = far_in_ref[:, here, :] + other.reshape(n, GROUP, ny)
        return 0

    lax.fori_loop(0, nx // 16, step, 0, unroll=True)


def copies_by_rows(source, target, done):
    rows = [slice(at, at + 16) for at in range(0, source.shape[1], 16)]
    return {r.start: pltpu.make_async_copy(source.at[:, r, :], target.at[:, r, :], done.at[i]) for i, r in enumerate(rows)}


def planes_from(first, core_ref, ref):
    at = jnp.where(core_ref[0] == 0, first[0], first[1])
    return lambda p: ref[at + p]


def ext_z(ext_ref, we, out_ref):
    n, nx, ny = out_ref.shape
    for at in range(0, nx, 2 * GROUP):
        block = ext_ref[:, at:at + 2 * GROUP, :].astype(F32)
        for half in range(2):
            ext = block[:, half * GROUP:(half + 1) * GROUP].reshape(n * GROUP, ny)
            ext = jnp.concatenate([ext, jnp.zeros((we[0].shape[1] - n * GROUP, ny), F32)], axis=0).astype(BF16)
            other = mul2(we, ext)
            here = slice(at + half * GROUP, at + (half + 1) * GROUP)
            out_ref[:, here, :] = other.reshape(n, GROUP, ny)


def to_quotient(load, recorded, more_ref, spread_ref, quotient_ref, wire_refs):
    mx, my = matrix(more_ref, X_FORWARD), matrix(more_ref, Y_FORWARD)
    pattern = tile_rows(spread_ref[...], quotient_ref.shape[1])
    for p in range(quotient_ref.shape[0]):
        quotient = recorded(p).astype(F32) / blur_rows(load(p), mx, my)
        quotient_ref[p] = quotient
        wire, at = (wire_refs[0], p) if p < wire_refs[0].shape[0] else (wire_refs[1], p - wire_refs[0].shape[0])
        wire[at] = (quotient * pattern).astype(BF16)


def to_log(load, count, m_ref, log_ref):
    mx, my = matrix(m_ref, X_ADJOINT), matrix(m_ref, Y_ADJOINT)
    views, _, rows, ny = log_ref.shape
    for p in range(count):
        log_ref[:, p] = jnp.log(blur_rows(load(p), mx, my)).reshape(views, rows, ny)


def first_far_kernel(first, core_ref, start_ref, sib_a_ref, sib_b_ref, more_ref, unspread_ref, recorded_ref, spread_ref,
                     quotient_ref, wire_ref, near_ref, far_ref, recorded, recorded_done, start, start_done):
    copies = copies_by_rows(start_ref, start, start_done)
    for copy in copies.values():
        copy.start()
    planes = pl.ds(jnp.where(core_ref[0] == 0, first[0], first[1]), recorded.shape[0])
    copy = pltpu.make_async_copy(recorded_ref.at[planes], recorded, recorded_done)
    copy.start()
    own, sib = matrix(more_ref, OWN_FORWARD), matrix(more_ref, SIB_FORWARD)
    fill_z([start], [sib_a_ref, sib_b_ref], own, sib, unspread_ref, far_ref, near_ref, before=lambda at: copies[at].wait())
    copy.wait()
    to_quotient(lambda p: far_ref[p], lambda p: recorded[p], more_ref, spread_ref, quotient_ref, [wire_ref])


def first_near_kernel(first, core_ref, near_ref, ext_ref, more_ref, unspread_ref, recorded_ref, spread_ref,
                      quotient_ref, wire_ref, sum_ref):
    ext_z(ext_ref, matrix(more_ref, EXT_FORWARD), sum_ref)
    recorded = planes_from(first, core_ref, recorded_ref)
    pattern = tile_rows(unspread_ref[...], sum_ref.shape[1])
    to_quotient(lambda p: near_ref[p] + sum_ref[p] * pattern, recorded, more_ref, spread_ref, quotient_ref, [wire_ref])


def block_kernel(block, first, core_ref, _, blocks_ref, more_ref, unspread_ref, recorded_ref, spread_ref, quotient_ref, *wire_refs):
    views, _, rows, ny = blocks_ref.shape
    pattern = tile_rows(unspread_ref[...], views * rows)

    def load(p):
        return blocks_ref[:, block + p].reshape(views * rows, ny).astype(F32) * pattern

    to_quotient(load, planes_from(first, core_ref, recorded_ref), more_ref, spread_ref, quotient_ref, wire_refs)


def adjoint_own_kernel(far_q_ref, near_q_ref, more_ref, spread_ref, far_ref, near_ref):
    fill_z([far_q_ref, near_q_ref], [], matrix(more_ref, OWN_ADJOINT), None, None, far_ref, near_ref, spread_ref)


def adjoint_far_kernel(far_in_ref, *refs):
    *sib_refs, m_ref, more_ref, unspread_ref, note_ref, log_ref, far_ref = refs
    add_sib(sib_refs, matrix(more_ref, SIB_ADJOINT), unspread_ref, far_in_ref, far_ref)
    to_log(lambda p: far_ref[p], far_ref.shape[0], m_ref, log_ref)
    for j in range(log_ref.shape[0] if log_ref.shape[1] > far_ref.shape[0] else 0):
        log_ref[j, far_ref.shape[0]] = note_ref[...]


def adjoint_near_kernel(near_ref, ext_ref, m_ref, unspread_ref, log_ref, sum_ref):
    ext_z(ext_ref, matrix(m_ref, EXT_ADJOINT), sum_ref)
    pattern = tile_rows(unspread_ref[...], sum_ref.shape[1])
    to_log(lambda p: (near_ref[p].astype(F32) + sum_ref[p]) * pattern, sum_ref.shape[0], m_ref, log_ref)


def rows_kernel(at, view_ref, volume_ref, _, __, far_ref, near_ref, arrived):
    core, first = view_ref[0], pl.multiple_of(view_ref[1] * far_ref.shape[1], far_ref.shape[1])
    copies = []
    for i, ref in enumerate((far_ref, near_ref)):
        planes = jnp.where(core == 0, at[i][0], at[i][1])
        source = volume_ref.at[pl.ds(planes, ref.shape[0]), pl.ds(first, ref.shape[1]), :]
        copies.append(pltpu.make_async_copy(source, ref, arrived.at[i]))
    for copy in copies:
        copy.start()
    for copy in copies:
        copy.wait()


def assemble_kernel(blocks_ref, out_ref, buffer, sent):
    depth, _, ny = out_ref.shape
    views, _, rows, _ = blocks_ref.shape
    step = depth // sent.shape[0]
    copies = []
    for z in range(depth):
        for j in range(views):
            exponent = blocks_ref[j, depth, z % rows:z % rows + 1, :]
            half = exponent[:, :ny // 2] if z < rows else exponent[:, ny // 2:]
            scale = jnp.exp2(jnp.concatenate([half, half], axis=1) - 15.0)
            buffer[z, j * rows:(j + 1) * rows] = blocks_ref[j, z] * scale
        if z % step == step - 1:
            part = slice(z + 1 - step, z + 1)
            copies.append(pltpu.make_async_copy(buffer.at[part], out_ref.at[part], sent.at[len(copies)]))
            copies[-1].start()
    for copy in copies:
        copy.wait()


def assemble(blocks, depth):
    views, _, rows, ny = blocks.shape
    shape = (depth, views * rows, ny)
    (out,) = call(assemble_kernel, [(shape, F32)], [blocks], [pltpu.VMEM(shape, F32), pltpu.SemaphoreType.DMA((8,))], hbm_out=(0,))
    return out


def to_other_chip(planes):
    count = lax.axis_size("gz")
    pairs = [(i, i + 1) for i in range(1, count - 1, 2)]
    return lax.ppermute(planes, "gz", pairs + [(b, a) for a, b in pairs])


def to_sibling(planes):
    count = lax.axis_size("gz")
    return lax.ppermute(planes, "gz", [(i, i ^ 1) for i in range(count)])


def to_views(blocks):
    return lax.all_to_all(blocks, "view", 0, 0)


def sum_over_x(log_blocks):
    views = lax.axis_size("view")
    groups = [list(range(z, views, 2)) for z in range(2)]
    blocks = log_blocks.reshape((views // 2, 2) + log_blocks.shape[1:])
    return lax.all_to_all(blocks, "view", 0, 0, axis_index_groups=groups)


def to_z_partner(block):
    return lax.ppermute(block, "view", [(i, i ^ 1) for i in range(lax.axis_size("view"))])


def band(kernel_row, out_pos, in_pos):
    tap_index = in_pos[None, :] - out_pos[:, None] + RADIUS
    one_hot = (tap_index[:, :, None] == jnp.arange(TAPS, dtype=jnp.int32)[None, None, :]).astype(F32)
    return jnp.sum(one_hot * kernel_row[None, None, :], axis=2)


def gather_result(piece):
    views = lax.axis_size("view")
    depth, rows, ny = piece.shape
    exponent = jnp.maximum(jnp.ceil(jnp.log2(jnp.max(piece, axis=(1, 2)))), -100.0)
    scaled = piece * jnp.exp2(15.0 - exponent)[:, None, None]
    note = jnp.broadcast_to(exponent.reshape(depth // rows, rows, 1), (depth // rows, rows, ny * rows // depth))
    note = jnp.concatenate(list(note), axis=1)[None]
    wire = jnp.concatenate([scaled, note], axis=0).astype(jnp.float16)
    return assemble(to_views(jnp.broadcast_to(wire[None], (views,) + wire.shape)).astype(F32), depth)


def per_device(views_data, psf, start):
    kernels = psf[0] / jnp.sum(psf[0], axis=1, keepdims=True)
    recorded = views_data[0]
    depth, nx, ny = recorded.shape
    views = lax.axis_size("view")
    v = lax.axis_index("view")
    core = lax.axis_index("gz") % 2
    z_lo = v % 2
    rows = nx // views
    n_near, n_far = RADIUS, depth - RADIUS
    spread, unspread = jnp.asarray(SPREAD), jnp.asarray(UNSPREAD)

    near_at, far_at = (depth - n_near) * core, (depth - n_far) * (1 - core)

    def to_wire(planes):
        count = planes.shape[-2] // spread.shape[0]
        return (planes * jnp.concatenate([spread] * count, axis=0)).astype(BF16)

    core_at = core.reshape(1).astype(jnp.int32)
    far_planes, near_planes = (depth - n_far, 0), (0, depth - n_near)
    n_sib = n_far - n_far // 2
    far_shape, near_shape = (n_far, nx, ny), (n_near, nx, ny)
    by_rows = pltpu.SemaphoreType.DMA((nx // 16,))
    sib_shapes = [((n_sib, nx, ny), BF16), ((n_far - n_sib, nx, ny), BF16)]

    (wire_near,) = call(
        lambda *refs: wire_kernel(near_planes, *refs),
        [(near_shape, BF16)],
        [core_at, start],
        [pltpu.VMEM(near_shape, F32), pltpu.SemaphoreType.DMA((3,))],
        smem=1, hbm=(1,),
    )
    ext = to_other_chip(wire_near)

    def matrices(rows, after):
        return call(
            lambda *refs: band_kernel(n_near, n_far, rows == KEPT_ROWS, *refs),
            [((rows, ny), F32)],
            [core_at, kernels, after],
            smem=2, anywhere=(2,),
        )[0]

    kept, more = matrices(KEPT_ROWS, wire_near), matrices(OTHER_ROWS, wire_near)
    sib = call(
        lambda core_ref, volume_ref, _, *refs: wire_kernel(far_planes, core_ref, volume_ref, *refs),
        sib_shapes,
        [core_at, start, wire_near],
        [pltpu.VMEM(far_shape, F32), pltpu.SemaphoreType.DMA((3,))],
        smem=1, anywhere=(2,), hbm=(1,),
    )
    sib = [to_sibling(wire) for wire in sib]

    quotient_far, wire_far, partly = call(
        lambda *refs: first_far_kernel(far_planes, *refs),
        [(far_shape, F32), (far_shape, BF16), (near_shape, F32)],
        [core_at, start, *sib, more, unspread, recorded, spread],
        [pltpu.VMEM(far_shape, F32), pltpu.VMEM(far_shape, BF16), pltpu.SemaphoreType.DMA, pltpu.VMEM(start.shape, F32), by_rows],
        smem=1, hbm=(1, 6),
    )
    sib = [to_sibling(wire_far)]
    quotient_near, wire_near = call(
        lambda *refs: first_near_kernel(near_planes, *refs),
        [(near_shape, F32), (near_shape, BF16)],
        [core_at, partly, ext, more, unspread, recorded, spread],
        [pltpu.VMEM(near_shape, F32)],
        smem=1, cost=HEAVY,
    )
    ext = to_other_chip(wire_near)

    count = jnp.arange(depth, dtype=jnp.int32)
    out_z = jnp.where(count < n_far, far_at + count, near_at + count - n_far)
    sib_z = count[:n_far] + jnp.where(core == 0, depth, -n_far)
    ext_z = count[:n_near] + jnp.where(core == 0, -n_near, depth)

    high = kernels[2].astype(jnp.float16).astype(F32)
    low = ((kernels[2] - high) * 2048.0).astype(jnp.float16).astype(F32)
    note = jnp.pad(jnp.stack([high, low]), ((0, rows - 2), (0, ny - TAPS)))

    for iteration in range(ITERS):
        extra = 1 if iteration == 0 else 0
        far_own, partly = call(
            adjoint_own_kernel,
            [(far_shape, F32), (near_shape, BF16)],
            [quotient_far, quotient_near, more, spread],
        )
        (log_far,) = call(
            adjoint_far_kernel,
            [((views, n_far + extra, rows, ny), F32)],
            [far_own, *sib, kept, more, unspread, note],
            [pltpu.VMEM(far_shape, F32)],
        )
        got = sum_over_x(log_far.astype(jnp.float16))

        (log_near,) = call(
            adjoint_near_kernel,
            [((views, n_near, rows, ny), F32)],
            [partly, ext, kept, unspread],
            [pltpu.VMEM(near_shape, F32)],
            cost=HEAVY,
        )
        log_near, got = lax.optimization_barrier((log_near.astype(jnp.float16), got))
        sums = jnp.sum(got[:, :, :n_far].astype(F32), axis=0)
        own_sum, other = jnp.where(z_lo == 0, sums[0], sums[1]), jnp.where(z_lo == 0, sums[1], sums[0])
        other = other.astype(jnp.float16)
        if iteration == 0:
            mine = got[:, 0, n_far, :2, :TAPS].reshape(views, TAPS)
            mine_planes = jnp.pad(mine, ((0, rows - views), (0, ny - TAPS)))[None]
            other = to_z_partner(jnp.concatenate([other, mine_planes], axis=0))
            pair = [mine.astype(F32), other[n_far, :views, :TAPS].astype(F32)]
            pair = [t.reshape(views // 2, 2, TAPS) for t in pair]
            pair = [t[:, 0] + t[:, 1] / 2048.0 for t in pair]
            every_z = jnp.where(z_lo == 0, jnp.stack(pair, axis=1), jnp.stack(pair[::-1], axis=1)).reshape(views, TAPS)
            other = other[:n_far]
            more = matrices(OTHER_ROWS, own_sum)
            piece_far, piece_near = call(
                lambda *refs: rows_kernel((far_planes, near_planes), *refs),
                [((n_far, rows, ny), F32), ((n_near, rows, ny), F32)],
                [jnp.stack([core, v]).astype(jnp.int32), start, own_sum, more],
                [pltpu.SemaphoreType.DMA((2,))],
                smem=1, anywhere=(2, 3), hbm=(1,),
            )
        else:
            other = to_z_partner(other)
        piece_far = piece_far * jnp.exp((own_sum + other.astype(F32)) / views)
        piece_near = piece_near * jnp.exp(jnp.sum(to_views(log_near).astype(F32), axis=0) / views)

        if iteration < ITERS - 1:
            wire_near = to_wire(piece_near)
            ext = to_other_chip(wire_near)
            piece_far, every_z, _ = lax.optimization_barrier((piece_far, every_z, wire_near))
            sib = to_sibling(to_wire(piece_far)).astype(F32) * unspread
            to_all = lambda planes, out, into: jnp.einsum(
                "zxy,voz->voxy", planes, jax.vmap(lambda row: band(row, out, into))(every_z), precision=lax.Precision.HIGH
            )
            planes = jnp.concatenate([piece_far, piece_near, sib, ext.astype(F32) * unspread], axis=0)
            blocks = to_wire(to_all(planes, out_z, jnp.concatenate([out_z, sib_z, ext_z])))
            blocks = to_views(blocks)
            quotient_near, wire_near = call(
                lambda *refs: block_kernel(n_far, near_planes, *refs),
                [(near_shape, F32), (near_shape, BF16)],
                [core_at, core_at, blocks, more, unspread, recorded, spread],
                smem=2, cost=HEAVY,
            )
            ext = to_other_chip(wire_near)
            quotient_far, wire_a, wire_b = call(
                lambda *refs: block_kernel(0, far_planes, *refs),
                [(far_shape, F32)] + sib_shapes,
                [core_at, wire_near, blocks, more, unspread, recorded, spread],
                smem=1, anywhere=(1,),
            )
            sib = [to_sibling(wire_a), to_sibling(wire_b)]

    both = jnp.concatenate([piece_near, piece_far, piece_near], axis=0)
    return gather_result(lax.dynamic_slice_in_dim(both, n_near * core, depth, axis=0))


def solution(mesh):
    in_specs = (P("view", "gz", None, None), P("view", None, None), P("gz", None, None))
    out_specs = P("gz", None, None)
    return jax.shard_map(
        per_device, mesh=mesh, in_specs=in_specs, out_specs=out_specs, check_vma=False
    )
```

```python
import math

import jax
import jax.numpy as jnp
import numpy as np
from jax import lax
from jax.experimental import pallas as pl
from jax.experimental.pallas import tpu as pltpu
from jax.sharding import PartitionSpec as P

RADIUS = 15
TAPS = 31
ITERS = 2
F32, BF16 = jnp.float32, jnp.bfloat16
GROUP = 8

ROW_STEP, COLUMN_STEP = 49471, 37345
_PHASE = np.arange(16)[:, None] * ROW_STEP + np.arange(256)[None, :] * COLUMN_STEP
SPREAD = (1.0 + (_PHASE % 65536) / 65536.0).astype(np.float32)
UNSPREAD = (1.0 / SPREAD.astype(np.float64)).astype(np.float32)


def spread_pattern(shape):
    row, column = lax.broadcasted_iota(jnp.int32, shape, 0), lax.broadcasted_iota(jnp.int32, shape, 1)
    return 1.0 + ((row * ROW_STEP + column * COLUMN_STEP) % 65536).astype(F32) / 65536.0


LIGHT = pl.CostEstimate(flops=1000, bytes_accessed=1000, transcendentals=0)
HEAVY = pl.CostEstimate(flops=6 * 10**10, bytes_accessed=2 * 10**8, transcendentals=0)


def call(kernel, outs, args, scratch=(), smem=0, anywhere=(), hbm=(), hbm_out=(), cost=LIGHT):
    held = sum(math.prod(a.shape) * jnp.dtype(a.dtype).itemsize for a in scratch if getattr(a, "memory_space", None) == pltpu.VMEM)
    anywhere = set(anywhere) | set(hbm)
    specs = [pl.BlockSpec(memory_space=pltpu.SMEM)] * smem
    specs += [pl.BlockSpec(memory_space=pl.ANY if i in anywhere else pltpu.VMEM) for i in range(smem, len(args))]
    args = [pltpu.with_memory_space_constraint(a, pltpu.HBM) if i in hbm else a for i, a in enumerate(args)]
    return pl.pallas_call(
        kernel,
        out_shape=[
            (pltpu.HBM if i in hbm_out else jax.ShapeDtypeStruct)(shape, dtype) for i, (shape, dtype) in enumerate(outs)
        ],
        in_specs=specs,
        out_specs=[
            pl.BlockSpec(memory_space=pl.ANY if i in hbm_out else pltpu.VMEM) for i in range(len(outs))
        ],
        scratch_shapes=list(scratch),
        compiler_params=pltpu.CompilerParams(vmem_limit_bytes=held + 3 * 1024 * 1024),
        cost_estimate=cost,
    )(*args)


def split(a):
    high = a.astype(BF16)
    return high, (a - high.astype(F32)).astype(BF16)


def mul(a, b):
    return jnp.dot(a, b, preferred_element_type=F32)


def mul3(a, b):
    return mul(a[0], b[0]) + mul(a[0], b[1]) + mul(a[1], b[0])


def mul2(a, b):
    return mul(jnp.concatenate(a, axis=1), jnp.concatenate([b, b], axis=0))


def tile_rows(pattern, rows):
    return jnp.concatenate([pattern] * (rows // pattern.shape[0]), axis=0)


X_ADJOINT, EXT_ADJOINT, Y_ADJOINT = (0, 0, 128, 128), (0, 128, 120, 128), (128, 0, 256, 256)
KEPT_ROWS = 384
Y_FORWARD = (0, 0, 256, 256)
OWN_FORWARD, OWN_ADJOINT = (256, 0, 256, 256), (512, 0, 256, 256)
SIB_FORWARD, SIB_ADJOINT = (768, 0, 136, 144), (904, 0, 136, 144)
X_FORWARD, EXT_FORWARD = (1040, 0, 128, 128), (1040, 128, 120, 128)
OTHER_ROWS = 1168


def matrix(ref, where):
    row, column, rows, columns = where
    return split(ref[row:row + rows, column:column + columns])


def band_kernel(n_near, n_far, kept, core_ref, taps_ref, _, out_ref):
    depth = n_near + n_far
    core = core_ref[0]
    near_at, far_at = (depth - n_near) * core, (depth - n_far) * (1 - core)
    natural = lambda i: i
    ordered = lambda i: jnp.where(i < n_far, far_at + i, near_at + i - n_far)
    near = lambda i: near_at + i
    ext = lambda i: i + jnp.where(core == 0, -n_near, depth)
    sib = lambda i: jnp.where(i < n_far, i + jnp.where(core == 0, depth, -n_far), 4 * depth)
    plans = [
        (X_ADJOINT, 0, natural, natural, -1, 1), (EXT_ADJOINT, 2, near, ext, -1, GROUP), (Y_ADJOINT, 1, natural, natural, 1, 1),
    ] if kept else [
        (Y_FORWARD, 1, natural, natural, -1, 1),
        (OWN_FORWARD, 2, ordered, natural, 1, GROUP), (OWN_ADJOINT, 2, ordered, ordered, -1, GROUP),
        (SIB_FORWARD, 2, ordered, sib, 1, GROUP), (SIB_ADJOINT, 2, ordered, sib, -1, GROUP),
        (X_FORWARD, 0, natural, natural, 1, 1), (EXT_FORWARD, 2, near, ext, 1, GROUP),
    ]
    for (at, column_at, rows, columns), axis, out_pos, in_pos, direction, repeat in plans:
        columns = -(-columns // 128) * 128
        row = lax.broadcasted_iota(jnp.int32, (rows, columns), 0)
        column = lax.broadcasted_iota(jnp.int32, (rows, columns), 1)
        tap = direction * (in_pos(column // repeat) - out_pos(row // repeat)) + RADIUS
        if repeat > 1:
            tap = jnp.where(row % repeat == column % repeat, tap, -1)
        total = jnp.zeros((rows, columns), F32)
        for k in range(TAPS):
            total = total + jnp.where(tap == k, taps_ref[axis, k], 0.0)
        out_ref[at:at + rows, column_at:column_at + columns] = total


def wire_kernel(at, core_ref, volume_ref, *refs):
    *wire_refs, buffer, arrived = refs
    first = jnp.where(core_ref[0] == 0, at[0], at[1])
    count, step = buffer.shape[0], -(-buffer.shape[0] // arrived.shape[0])
    parts = [slice(p, min(p + step, count)) for p in range(0, count, step)]
    copies = [
        pltpu.make_async_copy(volume_ref.at[pl.ds(first + r.start, r.stop - r.start)], buffer.at[r], arrived.at[i])
        for i, r in enumerate(parts)
    ]
    for copy in copies:
        copy.start()
    pattern = tile_rows(spread_pattern((16, buffer.shape[2])), buffer.shape[1])
    done = 0
    for wire_ref in wire_refs:
        for p in range(wire_ref.shape[0]):
            if done % step == 0:
                copies[done // step].wait()
            wire_ref[p] = (buffer[done] * pattern).astype(BF16)
            done += 1


def blur_rows(planes, mx, my):
    return mul3(split(mul3(mx, split(planes))), my)


def own_rows_z(own, wo):
    return mul3(wo, split(own))


def sib_rows_z(sib_refs, at, half, ws, unspread):
    sib = [r[:, pl.ds(at, 16), :].astype(F32)[:, half * GROUP:(half + 1) * GROUP] for r in sib_refs]
    sib = [a.reshape(a.shape[0] * GROUP, -1) for a in sib]
    rest = ws[0].shape[1] - sum(a.shape[0] for a in sib)
    sib = jnp.concatenate(sib + [jnp.zeros((rest, sib[0].shape[1]), F32)], axis=0).astype(BF16)
    other = mul(ws[0], sib) + mul(ws[1], sib)
    return other * tile_rows(unspread[half * GROUP:(half + 1) * GROUP], other.shape[0])


def fill_z(own_refs, sib_refs, wo, ws, unspread_ref, far_ref, near_ref, spread_ref=None, before=None):
    nx, ny = far_ref.shape[1:]
    cut = far_ref.shape[0] * GROUP
    for at in range(0, nx, 16):
        if before:
            before(at)
        near = []
        for half in range(2):
            here = slice(at + half * GROUP, at + (half + 1) * GROUP)
            own = jnp.concatenate([r[:, here, :].reshape(r.shape[0] * GROUP, ny) for r in own_refs], axis=0)
            out = own_rows_z(own, wo)
            far = out[:cut]
            if sib_refs:
                far = far + sib_rows_z(sib_refs, at, half, ws, unspread_ref[...])
            far_ref[:, here, :] = far.reshape(far_ref.shape[0], GROUP, ny)
            near.append(out[cut:].reshape(near_ref.shape[0], GROUP, ny))
        near = jnp.concatenate(near, axis=1)
        if spread_ref is not None:
            near = (near * spread_ref[...][None]).astype(BF16)
        near_ref[:, at:at + 16, :] = near


def add_sib(sib_refs, ws, unspread_ref, far_in_ref, far_ref):
    n, nx, ny = far_ref.shape

    def step(g, _):
        at = pl.multiple_of(g * 16, 16)
        for half in range(2):
            here = pl.ds(pl.multiple_of(at + half * GROUP, GROUP), GROUP)
            other = sib_rows_z(sib_refs, at, half, ws, unspread_ref[...])
            far_ref[:, here, :] = far_in_ref[:, here, :] + other.reshape(n, GROUP, ny)
        return 0

    lax.fori_loop(0, nx // 16, step, 0, unroll=True)


def copies_by_rows(source, target, done):
    rows = [slice(at, at + 16) for at in range(0, source.shape[1], 16)]
    return {r.start: pltpu.make_async_copy(source.at[:, r, :], target.at[:, r, :], done.at[i]) for i, r in enumerate(rows)}


def planes_from(first, core_ref, ref):
    at = jnp.where(core_ref[0] == 0, first[0], first[1])
    return lambda p: ref[at + p]


def ext_z(ext_ref, we, out_ref):
    n, nx, ny = out_ref.shape
    for at in range(0, nx, 2 * GROUP):
        block = ext_ref[:, at:at + 2 * GROUP, :].astype(F32)
        for half in range(2):
            ext = block[:, half * GROUP:(half + 1) * GROUP].reshape(n * GROUP, ny)
            ext = jnp.concatenate([ext, jnp.zeros((we[0].shape[1] - n * GROUP, ny), F32)], axis=0).astype(BF16)
            other = mul2(we, ext)
            here = slice(at + half * GROUP, at + (half + 1) * GROUP)
            out_ref[:, here, :] = other.reshape(n, GROUP, ny)


def to_quotient(load, recorded, more_ref, spread_ref, quotient_ref, wire_refs):
    mx, my = matrix(more_ref, X_FORWARD), matrix(more_ref, Y_FORWARD)
    pattern = tile_rows(spread_ref[...], quotient_ref.shape[1])
    for p in range(quotient_ref.shape[0]):
        quotient = recorded(p).astype(F32) / blur_rows(load(p), mx, my)
        quotient_ref[p] = quotient
        wire, at = (wire_refs[0], p) if p < wire_refs[0].shape[0] else (wire_refs[1], p - wire_refs[0].shape[0])
        wire[at] = (quotient * pattern).astype(BF16)


def to_log(load, count, m_ref, log_ref):
    mx, my = matrix(m_ref, X_ADJOINT), matrix(m_ref, Y_ADJOINT)
    views, _, rows, ny = log_ref.shape
    for p in range(count):
        log_ref[:, p] = jnp.log(blur_rows(load(p), mx, my)).reshape(views, rows, ny)


def first_far_kernel(first, core_ref, start_ref, sib_a_ref, sib_b_ref, more_ref, unspread_ref, recorded_ref, spread_ref,
                     quotient_ref, wire_ref, near_ref, far_ref, recorded, recorded_done, start, start_done):
    copies = copies_by_rows(start_ref, start, start_done)
    for copy in copies.values():
        copy.start()
    planes = pl.ds(jnp.where(core_ref[0] == 0, first[0], first[1]), recorded.shape[0])
    copy = pltpu.make_async_copy(recorded_ref.at[planes], recorded, recorded_done)
    copy.start()
    own, sib = matrix(more_ref, OWN_FORWARD), matrix(more_ref, SIB_FORWARD)
    fill_z([start], [sib_a_ref, sib_b_ref], own, sib, unspread_ref, far_ref, near_ref, before=lambda at: copies[at].wait())
    copy.wait()
    to_quotient(lambda p: far_ref[p], lambda p: recorded[p], more_ref, spread_ref, quotient_ref, [wire_ref])


def first_near_kernel(first, core_ref, near_ref, ext_ref, more_ref, unspread_ref, recorded_ref, spread_ref,
                      quotient_ref, wire_ref, sum_ref):
    ext_z(ext_ref, matrix(more_ref, EXT_FORWARD), sum_ref)
    recorded = planes_from(first, core_ref, recorded_ref)
    pattern = tile_rows(unspread_ref[...], sum_ref.shape[1])
    to_quotient(lambda p: near_ref[p] + sum_ref[p] * pattern, recorded, more_ref, spread_ref, quotient_ref, [wire_ref])


def block_kernel(block, first, core_ref, _, blocks_ref, more_ref, unspread_ref, recorded_ref, spread_ref, quotient_ref, *wire_refs):
    views, _, rows, ny = blocks_ref.shape
    pattern = tile_rows(unspread_ref[...], views * rows)

    def load(p):
        return blocks_ref[:, block + p].reshape(views * rows, ny).astype(F32) * pattern

    to_quotient(load, planes_from(first, core_ref, recorded_ref), more_ref, spread_ref, quotient_ref, wire_refs)


def adjoint_own_kernel(far_q_ref, near_q_ref, more_ref, spread_ref, far_ref, near_ref):
    fill_z([far_q_ref, near_q_ref], [], matrix(more_ref, OWN_ADJOINT), None, None, far_ref, near_ref, spread_ref)


def adjoint_far_kernel(far_in_ref, *refs):
    *sib_refs, m_ref, more_ref, unspread_ref, note_ref, log_ref, far_ref = refs
    add_sib(sib_refs, matrix(more_ref, SIB_ADJOINT), unspread_ref, far_in_ref, far_ref)
    to_log(lambda p: far_ref[p], far_ref.shape[0], m_ref, log_ref)
    for j in range(log_ref.shape[0] if log_ref.shape[1] > far_ref.shape[0] else 0):
        log_ref[j, far_ref.shape[0]] = note_ref[...]


def adjoint_near_kernel(near_ref, ext_ref, m_ref, unspread_ref, log_ref, sum_ref):
    ext_z(ext_ref, matrix(m_ref, EXT_ADJOINT), sum_ref)
    pattern = tile_rows(unspread_ref[...], sum_ref.shape[1])
    to_log(lambda p: (near_ref[p].astype(F32) + sum_ref[p]) * pattern, sum_ref.shape[0], m_ref, log_ref)


def rows_kernel(at, view_ref, volume_ref, _, __, far_ref, near_ref, arrived):
    core, first = view_ref[0], pl.multiple_of(view_ref[1] * far_ref.shape[1], far_ref.shape[1])
    copies = []
    for i, ref in enumerate((far_ref, near_ref)):
        planes = jnp.where(core == 0, at[i][0], at[i][1])
        source = volume_ref.at[pl.ds(planes, ref.shape[0]), pl.ds(first, ref.shape[1]), :]
        copies.append(pltpu.make_async_copy(source, ref, arrived.at[i]))
    for copy in copies:
        copy.start()
    for copy in copies:
        copy.wait()


def assemble_kernel(blocks_ref, out_ref, buffer, sent):
    depth, _, ny = out_ref.shape
    views, _, rows, _ = blocks_ref.shape
    step = depth // sent.shape[0]
    copies = []
    for z in range(depth):
        for j in range(views):
            exponent = blocks_ref[j, depth, z % rows:z % rows + 1, :]
            half = exponent[:, :ny // 2] if z < rows else exponent[:, ny // 2:]
            scale = jnp.exp2(jnp.concatenate([half, half], axis=1) - 15.0)
            buffer[z, j * rows:(j + 1) * rows] = blocks_ref[j, z] * scale
        if z % step == step - 1:
            part = slice(z + 1 - step, z + 1)
            copies.append(pltpu.make_async_copy(buffer.at[part], out_ref.at[part], sent.at[len(copies)]))
            copies[-1].start()
    for copy in copies:
        copy.wait()


def assemble(blocks, depth):
    views, _, rows, ny = blocks.shape
    shape = (depth, views * rows, ny)
    (out,) = call(assemble_kernel, [(shape, F32)], [blocks], [pltpu.VMEM(shape, F32), pltpu.SemaphoreType.DMA((8,))], hbm_out=(0,))
    return out


def to_other_chip(planes):
    count = lax.axis_size("gz")
    pairs = [(i, i + 1) for i in range(1, count - 1, 2)]
    return lax.ppermute(planes, "gz", pairs + [(b, a) for a, b in pairs])


def to_sibling(planes):
    count = lax.axis_size("gz")
    return lax.ppermute(planes, "gz", [(i, i ^ 1) for i in range(count)])


def to_views(blocks):
    return lax.all_to_all(blocks, "view", 0, 0)


def sum_over_x(log_blocks):
    views = lax.axis_size("view")
    groups = [list(range(z, views, 2)) for z in range(2)]
    blocks = log_blocks.reshape((views // 2, 2) + log_blocks.shape[1:])
    return lax.all_to_all(blocks, "view", 0, 0, axis_index_groups=groups)


def to_z_partner(block):
    return lax.ppermute(block, "view", [(i, i ^ 1) for i in range(lax.axis_size("view"))])


def band(kernel_row, out_pos, in_pos):
    tap_index = in_pos[None, :] - out_pos[:, None] + RADIUS
    one_hot = (tap_index[:, :, None] == jnp.arange(TAPS, dtype=jnp.int32)[None, None, :]).astype(F32)
    return jnp.sum(one_hot * kernel_row[None, None, :], axis=2)


def gather_result(piece):
    views = lax.axis_size("view")
    depth, rows, ny = piece.shape
    exponent = jnp.maximum(jnp.ceil(jnp.log2(jnp.max(piece, axis=(1, 2)))), -100.0)
    scaled = piece * jnp.exp2(15.0 - exponent)[:, None, None]
    note = jnp.broadcast_to(exponent.reshape(depth // rows, rows, 1), (depth // rows, rows, ny * rows // depth))
    note = jnp.concatenate(list(note), axis=1)[None]
    wire = jnp.concatenate([scaled, note], axis=0).astype(jnp.float16)
    return assemble(to_views(jnp.broadcast_to(wire[None], (views,) + wire.shape)).astype(F32), depth)


def per_device(views_data, psf, start):
    kernels = psf[0] / jnp.sum(psf[0], axis=1, keepdims=True)
    recorded = views_data[0]
    depth, nx, ny = recorded.shape
    views = lax.axis_size("view")
    v = lax.axis_index("view")
    core = lax.axis_index("gz") % 2
    z_lo = v % 2
    rows = nx // views
    n_near, n_far = RADIUS, depth - RADIUS
    spread, unspread = jnp.asarray(SPREAD), jnp.asarray(UNSPREAD)

    near_at, far_at = (depth - n_near) * core, (depth - n_far) * (1 - core)

    def to_wire(planes):
        count = planes.shape[-2] // spread.shape[0]
        return (planes * jnp.concatenate([spread] * count, axis=0)).astype(BF16)

    core_at = core.reshape(1).astype(jnp.int32)
    far_planes, near_planes = (depth - n_far, 0), (0, depth - n_near)
    n_sib = n_far - n_far // 2
    far_shape, near_shape = (n_far, nx, ny), (n_near, nx, ny)
    by_rows = pltpu.SemaphoreType.DMA((nx // 16,))
    sib_shapes = [((n_sib, nx, ny), BF16), ((n_far - n_sib, nx, ny), BF16)]

    (wire_near,) = call(
        lambda *refs: wire_kernel(near_planes, *refs),
        [(near_shape, BF16)],
        [core_at, start],
        [pltpu.VMEM(near_shape, F32), pltpu.SemaphoreType.DMA((3,))],
        smem=1, hbm=(1,),
    )
    ext = to_other_chip(wire_near)

    def matrices(rows, after):
        return call(
            lambda *refs: band_kernel(n_near, n_far, rows == KEPT_ROWS, *refs),
            [((rows, ny), F32)],
            [core_at, kernels, after],
            smem=2, anywhere=(2,),
        )[0]

    kept, more = matrices(KEPT_ROWS, wire_near), matrices(OTHER_ROWS, wire_near)
    sib = call(
        lambda core_ref, volume_ref, _, *refs: wire_kernel(far_planes, core_ref, volume_ref, *refs),
        sib_shapes,
        [core_at, start, wire_near],
        [pltpu.VMEM(far_shape, F32), pltpu.SemaphoreType.DMA((3,))],
        smem=1, anywhere=(2,), hbm=(1,),
    )
    sib = [to_sibling(wire) for wire in sib]

    quotient_far, wire_far, partly = call(
        lambda *refs: first_far_kernel(far_planes, *refs),
        [(far_shape, F32), (far_shape, BF16), (near_shape, F32)],
        [core_at, start, *sib, more, unspread, recorded, spread],
        [pltpu.VMEM(far_shape, F32), pltpu.VMEM(far_shape, BF16), pltpu.SemaphoreType.DMA, pltpu.VMEM(start.shape, F32), by_rows],
        smem=1, hbm=(1, 6),
    )
    sib = [to_sibling(wire_far)]
    quotient_near, wire_near = call(
        lambda *refs: first_near_kernel(near_planes, *refs),
        [(near_shape, F32), (near_shape, BF16)],
        [core_at, partly, ext, more, unspread, recorded, spread],
        [pltpu.VMEM(near_shape, F32)],
        smem=1, cost=HEAVY,
    )
    ext = to_other_chip(wire_near)

    count = jnp.arange(depth, dtype=jnp.int32)
    out_z = jnp.where(count < n_far, far_at + count, near_at + count - n_far)
    sib_z = count[:n_far] + jnp.where(core == 0, depth, -n_far)
    ext_z = count[:n_near] + jnp.where(core == 0, -n_near, depth)

    high = kernels[2].astype(jnp.float16).astype(F32)
    low = ((kernels[2] - high) * 2048.0).astype(jnp.float16).astype(F32)
    note = jnp.pad(jnp.stack([high, low]), ((0, rows - 2), (0, ny - TAPS)))

    for iteration in range(ITERS):
        extra = 1 if iteration == 0 else 0
        far_own, partly = call(
            adjoint_own_kernel,
            [(far_shape, F32), (near_shape, BF16)],
            [quotient_far, quotient_near, more, spread],
        )
        (log_far,) = call(
            adjoint_far_kernel,
            [((views, n_far + extra, rows, ny), F32)],
            [far_own, *sib, kept, more, unspread, note],
            [pltpu.VMEM(far_shape, F32)],
        )
        got = sum_over_x(log_far.astype(jnp.float16))

        (log_near,) = call(
            adjoint_near_kernel,
            [((views, n_near, rows, ny), F32)],
            [partly, ext, kept, unspread],
            [pltpu.VMEM(near_shape, F32)],
            cost=HEAVY,
        )
        log_near, got = lax.optimization_barrier((log_near.astype(jnp.float16), got))
        sums = jnp.sum(got[:, :, :n_far].astype(F32), axis=0)
        own_sum, other = jnp.where(z_lo == 0, sums[0], sums[1]), jnp.where(z_lo == 0, sums[1], sums[0])
        other = other.astype(jnp.float16)
        if iteration == 0:
            mine = got[:, 0, n_far, :2, :TAPS].reshape(views, TAPS)
            mine_planes = jnp.pad(mine, ((0, rows - views), (0, ny - TAPS)))[None]
            other = to_z_partner(jnp.concatenate([other, mine_planes], axis=0))
            pair = [mine.astype(F32), other[n_far, :views, :TAPS].astype(F32)]
            pair = [t.reshape(views // 2, 2, TAPS) for t in pair]
            pair = [t[:, 0] + t[:, 1] / 2048.0 for t in pair]
            every_z = jnp.where(z_lo == 0, jnp.stack(pair, axis=1), jnp.stack(pair[::-1], axis=1)).reshape(views, TAPS)
            other = other[:n_far]
            more = matrices(OTHER_ROWS, own_sum)
            piece_far, piece_near = call(
                lambda *refs: rows_kernel((far_planes, near_planes), *refs),
                [((n_far, rows, ny), F32), ((n_near, rows, ny), F32)],
                [jnp.stack([core, v]).astype(jnp.int32), start, own_sum, more],
                [pltpu.SemaphoreType.DMA((2,))],
                smem=1, anywhere=(2, 3), hbm=(1,),
            )
        else:
            other = to_z_partner(other)
        piece_far = piece_far * jnp.exp((own_sum + other.astype(F32)) / views)
        piece_near = piece_near * jnp.exp(jnp.sum(to_views(log_near).astype(F32), axis=0) / views)

        if iteration < ITERS - 1:
            wire_near = to_wire(piece_near)
            ext = to_other_chip(wire_near)
            piece_far, every_z, _ = lax.optimization_barrier((piece_far, every_z, wire_near))
            sib = to_sibling(to_wire(piece_far)).astype(F32) * unspread
            to_all = lambda planes, out, into: jnp.einsum(
                "zxy,voz->voxy", planes, jax.vmap(lambda row: band(row, out, into))(every_z), precision=lax.Precision.HIGH
            )
            planes = jnp.concatenate([piece_far, piece_near, sib, ext.astype(F32) * unspread], axis=0)
            blocks = to_wire(to_all(planes, out_z, jnp.concatenate([out_z, sib_z, ext_z])))
            blocks = to_views(blocks)
            quotient_near, wire_near = call(
                lambda *refs: block_kernel(n_far, near_planes, *refs),
                [(near_shape, F32), (near_shape, BF16)],
                [core_at, core_at, blocks, more, unspread, recorded, spread],
                smem=2, cost=HEAVY,
            )
            ext = to_other_chip(wire_near)
            quotient_far, wire_far = call(
                lambda *refs: block_kernel(0, far_planes, *refs),
                [(far_shape, F32), (far_shape, BF16)],
                [core_at, wire_near, blocks, more, unspread, recorded, spread],
                smem=1, anywhere=(1,),
            )
            sib = [to_sibling(wire_far)]

    both = jnp.concatenate([piece_near, piece_far, piece_near], axis=0)
    return gather_result(lax.dynamic_slice_in_dim(both, n_near * core, depth, axis=0))


def solution(mesh):
    in_specs = (P("view", "gz", None, None), P("view", None, None), P("gz", None, None))
    out_specs = P("gz", None, None)
    return jax.shard_map(
        per_device, mesh=mesh, in_specs=in_specs, out_specs=out_specs, check_vma=False
    )
```
